128 devices in a mesh: lat: 8 (over y_hi, x), lon: 16 (over z, y_lo, core).
Axes of the slice: x: 4, y: 4 (y_hi: 2, y_lo: 2; y = y_hi * 2 + y_lo), z: 4, core: 2. Of those that a mesh axis runs over, the one named last changes fastest.
Arguments:
- station_tile: int32 [65536, 1], P(('lat', 'lon')), may hold values from 0 to 127; in each aligned block of 512 rows (0 to 511, 512 to 1023, ...) at most 8 rows name the same one
- station_cell: int32 [65536], P(('lat', 'lon')), may hold values from 0 to 8191
- station_offset: float32 [2, 65536], P(None, ('lat', 'lon')), may hold values from -0.5 to 0.5
- station_values: float32 [4, 65536], P(None, ('lat', 'lon')), may hold values from -6 to 6
- covariates: bfloat16 [8, 512, 2048], P(None, 'lat', 'lon'), may hold values from -6 to 6
- target_tile: int32 [32768, 1], P(('lat', 'lon')), may hold values from 0 to 127; in each aligned block of 256 rows (0 to 255, 256 to 511, ...) at most 4 rows name the same one
- target_cell: int32 [32768], P(('lat', 'lon')), may hold values from 0 to 8191
- target_offset: float32 [2, 32768], P(None, ('lat', 'lon')), may hold values from -0.5 to 0.5
- lift_weight: bfloat16 [13, 64], replicated, may hold values from -1.75 to 1.75
- first_kernel: bfloat16 [64, 1600], replicated, may hold values from -0.15625 to 0.15625
- second_kernel: bfloat16 [64, 1600], replicated, may hold values from -0.15625 to 0.15625
- out_weight: float32 [64, 2], replicated, may hold values from -0.75 to 0.75
- cotangent: float32 [2, 32768], P(None, ('lat', 'lon')), may hold values from -0.046875 to 0.046875
Outputs:
- predictions: float32 [2, 32768], P(None, ('lat', 'lon'))
- grad_lift: float32 [13, 64], replicated
- grad_first: float32 [64, 1600], replicated
- grad_second: float32 [64, 1600], replicated
- grad_out: float32 [64, 2], replicated
The draws below stay inside these ranges and needn't reach their ends.
Inputs may be any that keep to these rules, and one draw needn't show every extreme that they name: `station_tile`: tiles are numbered band * 16 + column tile. Among the rows of one device no tile is named more than 8 times. `target_tile`: tiles are numbered as for stations. Among the rows of one device no tile is named more than 4 times.
All inputs are finite; a program needn't handle non-finite values.
Results may differ from the reference program's by a relative error of at most 0.0034.
The reference program's roundings to bfloat16 on the way count: a program that leaves them out, or rounds other values in their place, can miss the bound.
Values may be sent and summed in bfloat16 or wider, within the bound.
No kernel may reach another device: no remote copies, remote signals or barrier semaphores. Data moves between devices by JAX's collectives and lax.ppermute only.
A program may use at most 320 MiB of HBM per device.

```python
import math
import jax
import jax.numpy as jnp
import numpy as np
from jax import lax

CHANNELS = 64
VARS = 4
COVARS = 8
OUTPUTS = 2
KERNEL = 5
REACH = 4
ROWS = 64
COLS = 128
STN_DEV = 512
TGT_DEV = 256
STN_CAP = 8
TGT_CAP = 4
STATIONS = 65536
TARGETS = 32768
GRID_ROWS = 512
GRID_COLS = 2048
N_LAT = 8
N_LON = 16
DEVICES = 128


def touch_ends(result, own_key, least, largest):
    longest = result.shape.index(max(result.shape))
    spots = []
    for shift in (0, 1):
        where = [jax.random.randint(jax.random.fold_in(own_key, axis), (), 0, length) for axis, length in enumerate(result.shape)]
        where[longest] = (where[longest] + shift) % result.shape[longest]
        spots.append(tuple(where))
    return result.at[spots[0]].set(least).at[spots[1]].set(largest)


def block_levels(key, shape, split, low, largest):
    def one(dim, parts):
        steps = jax.random.uniform(jax.random.fold_in(jax.random.fold_in(key, 6), dim), (parts,), jnp.float32, low / len(split), largest / len(split))
        return jnp.repeat(jnp.exp(steps), shape[dim] // parts).reshape((-1,) + (1,) * (len(shape) - dim - 1))

    loudness = one(*split[0])
    for cut in split[1:]:
        loudness = loudness * one(*cut)
    return loudness


def routed_block(rng, own, number, rows, number_of, top, limit, slope):
    order = jax.random.permutation(rng, number_of)
    crowded, common = shares(number_of, rows * top, limit, slope, True), shares(number_of, rows * top, limit, slope, False)
    places = jnp.arange(number_of)

    def named(lengths, rotation):
        used = int((lengths > 0).sum())
        fixed = max(1, used // 4)
        moved = fixed + (places - fixed + rotation * (used - fixed)) % max(1, number_of - fixed)
        return jnp.zeros((number_of,), jnp.int32).at[order[jnp.where(places < fixed, places, moved)]].set(jnp.asarray(lengths, jnp.int32))

    lengths = jnp.where(number % 4 == 0, named(crowded, number // 4), named(common, number - number // 4 - 1))
    mixed = jax.random.permutation(jax.random.fold_in(own, 3), number_of)
    donor, taker = mixed[0:number_of // 2 * 2:2], mixed[1:number_of // 2 * 2:2]
    room = jnp.minimum(lengths[donor] - 1, limit - lengths[taker]) // 2
    room = jnp.where((donor == order[0]) | (taker == order[0]) | (lengths[taker] == 0), 0, jnp.maximum(room, 0))
    moved = jax.random.randint(jax.random.fold_in(own, 4), (number_of // 2,), 0, 1 << 20) % (room + 1)
    lengths = lengths.at[donor].add(-moved).at[taker].add(moved)
    items = jnp.searchsorted(jnp.cumsum(lengths), jnp.arange(rows * top), side="right").astype(jnp.int32)
    listing = items.reshape(top, rows).T
    listing = listing[jax.random.permutation(jax.random.fold_in(own, 1), rows)]
    rotation = jax.random.randint(jax.random.fold_in(own, 2), (rows, 1), 0, top)
    return jnp.take_along_axis(listing, (jnp.arange(top)[None, :] + rotation) % top, axis=1)


def shares(number_of, total, reach, lean, full):
    loads = [(1 << 20) // math.isqrt(standing ** lean) + 1 for standing in range(1, number_of + 1)]
    largest = reach if full else min(reach, max(-(-total // number_of), total * loads[0] // sum(loads)))
    least = 1 if total - largest >= number_of - 1 else 0
    given, surplus = [largest] + [least] * (number_of - 1), total - largest - least * (number_of - 1)
    while surplus > 0:
        candidates = [i for i in range(1, number_of) if given[i] < largest] or [i for i in range(1, number_of) if given[i] < reach]
        mass, remaining = sum([loads[i] for i in candidates]), surplus
        for i in candidates:
            addition = min(reach - given[i], max(1, remaining * loads[i] // mass), surplus)
            given[i] = given[i] + addition
            surplus = surplus - addition
    return np.array(given)


def normal_values(stream_key, dims, spread, bound, cuts=(), kind=jnp.bfloat16):
    values = jax.random.normal(stream_key, dims, jnp.float32) * spread
    if len(cuts) > 0:
        values = block_levels(stream_key, dims, cuts, -0.22, 0.18) * values
    return jnp.clip(values, min=-bound, max=bound).astype(kind)


def setup_inputs(seed: int = 0) -> dict:
    keys = jax.random.split(jax.random.key(seed), 14)
    station_tile_keys = jax.random.split(jax.random.fold_in(keys[0], 1), STATIONS // STN_DEV)
    station_tile_turns = jax.random.permutation(jax.random.fold_in(keys[0], 3), STATIONS // STN_DEV)
    station_tile = jax.vmap(lambda own, number: routed_block(jax.random.fold_in(keys[0], 2), own, number, STN_DEV, DEVICES, 1, STN_CAP, 2))(station_tile_keys, station_tile_turns).reshape((STATIONS, 1))
    station_cell = touch_ends(jax.random.randint(keys[1], (STATIONS,), 0, ROWS * COLS), jax.random.fold_in(keys[1], 1), 0, (ROWS * COLS) - 1).astype(jnp.int32)
    station_offset = jnp.clip(jax.random.uniform(keys[2], (2, STATIONS), jnp.float32, -0.5, 0.5) * block_levels(keys[2], (2, STATIONS), ((1, 128),), -0.4, 0.0), -0.5, 0.5)
    station_values = normal_values(keys[3], (VARS, STATIONS), 1.0, 6.0, ((1, 128),), jnp.float32)
    covariates = normal_values(keys[4], (COVARS, GRID_ROWS, GRID_COLS), 1.0, 6.0, ((1, 8), (2, 16)))
    target_tile_keys = jax.random.split(jax.random.fold_in(keys[5], 1), TARGETS // TGT_DEV)
    target_tile_turns = jax.random.permutation(jax.random.fold_in(keys[5], 3), TARGETS // TGT_DEV)
    target_tile = jax.vmap(lambda own, number: routed_block(jax.random.fold_in(keys[5], 2), own, number, TGT_DEV, DEVICES, 1, TGT_CAP, 2))(target_tile_keys, target_tile_turns).reshape((TARGETS, 1))
    target_cell = touch_ends(jax.random.randint(keys[6], (TARGETS,), 0, ROWS * COLS), jax.random.fold_in(keys[6], 1), 0, (ROWS * COLS) - 1).astype(jnp.int32)
    target_offset = jnp.clip(jax.random.uniform(keys[7], (2, TARGETS), jnp.float32, -0.5, 0.5) * block_levels(keys[7], (2, TARGETS), ((1, 128),), -0.4, 0.0), -0.5, 0.5)
    lift_weight = normal_values(keys[8], (VARS + 1 + COVARS, CHANNELS), (VARS + 1 + COVARS) ** -0.5, 1.75)
    first_kernel = normal_values(keys[9], (CHANNELS, CHANNELS * KERNEL * KERNEL), (CHANNELS * KERNEL * KERNEL) ** -0.5, 0.15625)
    second_kernel = normal_values(keys[10], (CHANNELS, CHANNELS * KERNEL * KERNEL), (CHANNELS * KERNEL * KERNEL) ** -0.5, 0.15625)
    out_weight = normal_values(keys[11], (CHANNELS, OUTPUTS), CHANNELS ** -0.5, 0.75, (), jnp.float32)
    cotangent = normal_values(keys[12], (OUTPUTS, TARGETS), 0.003, 0.046875, ((1, 128),), jnp.float32)
    return {"station_tile": station_tile, "station_cell": station_cell, "station_offset": station_offset, "station_values": station_values, "covariates": covariates, "target_tile": target_tile, "target_cell": target_cell, "target_offset": target_offset, "lift_weight": lift_weight, "first_kernel": first_kernel, "second_kernel": second_kernel, "out_weight": out_weight, "cotangent": cotangent}


inverse_width = 1.0 / 4.5


def highest_dot(first_arg, second_arg):
    return jnp.dot(first_arg, second_arg, precision=lax.Precision.HIGHEST, preferred_element_type=jnp.float32)


def window_factor(offset):
    steps_int = jnp.arange(-REACH, REACH + 1, dtype=jnp.int32)
    distance = steps_int.astype(jnp.float32)[None, :] - offset[:, None]
    return jnp.exp(-(distance * distance) * inverse_width)


def bucket(tile_ids, columns, capacity):
    tile_total = N_LAT * N_LON
    order = jnp.argsort(tile_ids, stable=True).astype(jnp.int32)
    ordered = tile_ids[order]
    counts = jnp.sum((tile_ids[:, None] == jnp.arange(tile_total, dtype=jnp.int32)[None, :]).astype(jnp.int32), axis=0).astype(jnp.int32)
    starts = (jnp.cumsum(counts) - counts).astype(jnp.int32)
    sorted_rank = jnp.arange(tile_ids.shape[0], dtype=jnp.int32) - starts[ordered]
    table = jnp.zeros((tile_total, capacity, columns.shape[0]), columns.dtype)
    table = table.at[ordered, sorted_rank].set(columns[:, order].T)
    rank_of = jnp.zeros(tile_ids.shape, jnp.int32).at[order].set(sorted_rank)
    return jnp.transpose(table, (0, 2, 1)), rank_of


def tile_spread(row_ids, col_ids, down, across, amounts):
    span = 2 * REACH + 1
    grid_part = jnp.zeros((ROWS + 2 * REACH, COLS + 2 * REACH, amounts.shape[0]), jnp.float32)
    row_index = row_ids[:, None, None] + jnp.arange(span, dtype=jnp.int32)[None, :, None]
    col_index = col_ids[:, None, None] + jnp.arange(span, dtype=jnp.int32)[None, None, :]
    weights = down[:, :, None] * across[:, None, :]
    terms = weights[:, :, :, None] * amounts.T[:, None, None, :]
    grid_part = grid_part.at[row_index, col_index].add(terms)
    return jnp.transpose(grid_part, (2, 0, 1))


def assemble(part_of, channels, extras_init):
    span_rows = ROWS + 2 * REACH
    span_cols = COLS + 2 * REACH
    row_line = jnp.arange(span_rows)
    col_line = jnp.arange(span_cols)
    inside = ((row_line >= REACH) & (row_line < ROWS + REACH))[:, None] & ((col_line >= REACH) & (col_line < COLS + REACH))[None, :]
    canvas = jnp.zeros((channels, GRID_ROWS + 2 * REACH, GRID_COLS + 2 * REACH), jnp.float32)

    def place(tile_id, loop_state):
        canvas_now, extras = loop_state
        tile_id = tile_id.astype(jnp.int32)
        tile_part, extras = part_of(tile_id, extras)
        rounded = lax.optimization_barrier(tile_part.astype(jnp.bfloat16)).astype(jnp.float32)
        tile_part = jnp.where(inside[None], tile_part, rounded)
        corner_at = (jnp.zeros((), jnp.int32), ((tile_id // N_LON) * ROWS).astype(jnp.int32), ((tile_id % N_LON) * COLS).astype(jnp.int32))
        old_part = lax.dynamic_slice(canvas_now, corner_at, (channels, span_rows, span_cols))
        return lax.dynamic_update_slice(canvas_now, old_part + tile_part, corner_at), extras

    canvas, extras = lax.fori_loop(0, N_LAT * N_LON, place, (canvas, extras_init))
    inner_rows = canvas[:, REACH:REACH + GRID_ROWS, :]
    core = inner_rows[:, :, REACH:REACH + GRID_COLS]
    core = core.at[:, :, GRID_COLS - REACH:].add(inner_rows[:, :, :REACH])
    core = core.at[:, :, :REACH].add(inner_rows[:, :, GRID_COLS + REACH:])
    return core, extras


def wrap_pad(tensor, margin):
    tensor = jnp.concatenate([tensor[:, :, tensor.shape[2] - margin:], tensor, tensor[:, :, :margin]], axis=2)
    return jnp.pad(tensor, ((0, 0), (margin, margin), (0, 0)))


def convolve(tensor, kernel):
    padded = wrap_pad(tensor, KERNEL // 2).astype(jnp.float32)
    weights = kernel.reshape(kernel.shape[0], -1, KERNEL, KERNEL).astype(jnp.float32)
    return lax.conv_general_dilated(padded[None], weights, (1, 1), "VALID", dimension_numbers=("NCHW", "OIHW", "NCHW"), precision=lax.Precision.HIGHEST)[0]


def flipped(kernel):
    out_count = kernel.shape[0]
    shaped = kernel.reshape(out_count, -1, KERNEL, KERNEL)
    turned = jnp.transpose(shaped, (1, 0, 2, 3))[:, :, ::-1, ::-1]
    return turned.reshape(turned.shape[0], out_count * KERNEL * KERNEL)


def correlate(tensor, grads):
    padded = wrap_pad(tensor, KERNEL // 2)
    left_side = grads.reshape(grads.shape[0], -1).astype(jnp.float32)
    pieces = []
    for row_shift in range(KERNEL):
        for col_shift in range(KERNEL):
            window = padded[:, row_shift:row_shift + GRID_ROWS, col_shift:col_shift + GRID_COLS]
            window = window.reshape(tensor.shape[0], -1).astype(jnp.float32)
            pieces.append(highest_dot(left_side, window.T))
    return jnp.stack(pieces, axis=2).reshape(grads.shape[0], -1)


def reference(station_tile, station_cell, station_offset, station_values, covariates, target_tile, target_cell, target_offset, lift_weight, first_kernel, second_kernel, out_weight, cotangent):
    span = 2 * REACH + 1
    tile_total = N_LAT * N_LON
    station_ids = station_tile[:, 0]
    station_columns = jnp.concatenate([
        (station_cell // COLS).astype(jnp.float32)[None],
        (station_cell % COLS).astype(jnp.float32)[None],
        station_offset,
        jnp.ones((1, station_ids.shape[0]), jnp.float32),
        station_values], axis=0)
    station_table, station_rank = bucket(station_ids, station_columns, 4 * STN_DEV)

    def density_part(tile_id, extras):
        columns = station_table[tile_id]
        row_ids = columns[0].astype(jnp.int32)
        col_ids = columns[1].astype(jnp.int32)
        down = window_factor(columns[2])
        across = window_factor(columns[3])
        return tile_spread(row_ids, col_ids, down, across, columns[4:]), extras

    density, unused_extras = assemble(density_part, VARS + 1, jnp.zeros((), jnp.float32))
    density_zero = density[0]
    features = jnp.concatenate([density_zero[None], density[1:] / jnp.maximum(density_zero, 1.0)[None]], axis=0).astype(jnp.bfloat16)
    stacked = jnp.concatenate([features, covariates], axis=0)
    lifted = jnp.einsum("kc,kij->cij", lift_weight.astype(jnp.float32), stacked.astype(jnp.float32), precision=lax.Precision.HIGHEST).astype(jnp.bfloat16)
    hidden = jnp.maximum(convolve(lifted, first_kernel), 0.0).astype(jnp.bfloat16)
    latent = (lifted.astype(jnp.float32) + convolve(hidden, second_kernel)).astype(jnp.bfloat16)
    latent_pad = wrap_pad(latent, REACH)

    target_ids = target_tile[:, 0]
    target_columns = jnp.concatenate([
        (target_cell // COLS).astype(jnp.float32)[None],
        (target_cell % COLS).astype(jnp.float32)[None],
        target_offset,
        cotangent], axis=0)
    target_table, target_rank = bucket(target_ids, target_columns, 4 * TGT_DEV)

    def latent_part(tile_id, extras):
        answers, grad_sum = extras
        columns = target_table[tile_id]
        row_ids = columns[0].astype(jnp.int32)
        col_ids = columns[1].astype(jnp.int32)
        corner_at = (jnp.zeros((), jnp.int32), ((tile_id // N_LON) * ROWS).astype(jnp.int32), ((tile_id % N_LON) * COLS).astype(jnp.int32))
        local_grid = lax.dynamic_slice(latent_pad, corner_at, (CHANNELS, ROWS + 2 * REACH, COLS + 2 * REACH)).astype(jnp.float32)
        down = window_factor(columns[2])
        across = lax.optimization_barrier(window_factor(columns[3]).astype(jnp.bfloat16)).astype(jnp.float32)

        def one_window(row_at, col_at):
            return lax.dynamic_slice(local_grid, (jnp.zeros((), jnp.int32), row_at, col_at), (CHANNELS, span, span))

        windows = jax.vmap(one_window)(row_ids, col_ids)
        decoded = jnp.einsum("scuv,su,sv->cs", windows, down, across, precision=lax.Precision.HIGHEST)
        cotan = columns[4:]
        tile_predictions = highest_dot(out_weight.T, decoded)
        grad_sum = grad_sum + highest_dot(decoded, cotan.T)
        back = highest_dot(out_weight, cotan)
        tile_part = tile_spread(row_ids, col_ids, down, across, back)
        answers = answers.at[tile_id].set(tile_predictions)
        return tile_part, (answers, grad_sum)

    answers_init = jnp.zeros((tile_total, OUTPUTS, 4 * TGT_DEV), jnp.float32)
    grad_init = jnp.zeros((CHANNELS, OUTPUTS), jnp.float32)
    latent_grad_sum, (answers, grad_out) = assemble(latent_part, CHANNELS, (answers_init, grad_init))
    latent_grad = latent_grad_sum.astype(jnp.bfloat16)
    predictions = answers[target_ids, :, target_rank].T

    hidden_grad = (convolve(latent_grad, flipped(second_kernel)) * (hidden > 0)).astype(jnp.bfloat16)
    grad_second = correlate(hidden, latent_grad)
    lifted_grad = latent_grad.astype(jnp.float32) + convolve(hidden_grad, flipped(first_kernel))
    grad_first = correlate(lifted, hidden_grad)
    grad_lift = highest_dot(stacked.reshape(stacked.shape[0], -1).astype(jnp.float32), lifted_grad.reshape(CHANNELS, -1).T)
    return predictions, grad_lift, grad_first, grad_second, grad_out
```

```python
import functools

import jax
import jax.numpy as jnp
import numpy as np
from jax import lax
from jax.experimental import pallas as pl
from jax.experimental.pallas import tpu as pltpu
from jax.sharding import PartitionSpec as P

KERNEL = 5
REACH = 4
INV = 1.0 / 4.5
F32 = jnp.float32
BF16 = jnp.bfloat16
BANDS = 8
LONS = 16
TILES = 128
OFFS = ((-1, -1), (-1, 0), (-1, 1), (0, -1), (0, 1), (1, -1), (1, 0), (1, 1), (0, 0))
NT = (((1,), (1,)), ((), ()))
NN = (((1,), (0,)), ((), ()))


def dot(a, b, dims=NN):
    return lax.dot_general(a, b, dims, preferred_element_type=F32)


def iota(shape, axis):
    return lax.broadcasted_iota(jnp.int32, shape, axis)


def split2(x):
    hi = x.astype(BF16)
    return hi, (x - hi.astype(F32)).astype(BF16)


def split3(x):
    hi = x.astype(BF16)
    rest = x - hi.astype(F32)
    mid = rest.astype(BF16)
    return hi, mid, (rest - mid.astype(F32)).astype(BF16)


def rounded(x):
    return x.astype(BF16).astype(F32)


def as_bf16(mask):
    return mask.astype(F32).astype(BF16)


def ranked(tile_row):
    count = tile_row.shape[1]
    hits = iota((TILES, count), 0) == tile_row
    earlier = as_bf16(iota((count, count), 0) < iota((count, count), 1))
    hits_b = as_bf16(hits)
    before = dot(hits_b, earlier)
    rank = jnp.sum(jnp.where(hits, before, 0.0), axis=0, keepdims=True)
    return hits_b, rank


def pack_kernel(st_tile, st_rec, tg_tile, tg_rec, send, tg_rank):
    s_hits, s_rank = ranked(st_tile[...])
    t_hits, t_rank = ranked(tg_tile[...])
    tg_rank[...] = jnp.broadcast_to(t_rank, tg_rank.shape)
    n_s, n_t = s_rank.shape[1], t_rank.shape[1]
    s_rec, t_rec = st_rec[...], tg_rec[...]
    s_rows = jnp.concatenate([jnp.where(s_rank == k, s_rec, 0.0) for k in range(8)], axis=0)
    t_rows = jnp.concatenate([jnp.where(t_rank == k, t_rec, 0.0) for k in range(4)], axis=0)
    s_rows = jnp.concatenate([s_rows, jnp.zeros((64, n_s), F32)], axis=0)
    t_rows = jnp.concatenate(
        [jnp.zeros((64, n_t), F32), t_rows, jnp.zeros((32, n_t), F32)], axis=0
    )
    hits = jnp.concatenate([s_hits, t_hits], axis=1)
    rows = jnp.concatenate([s_rows, t_rows], axis=1)
    bucket = sum(dot(hits, part, NT) for part in split3(rows))
    parts = split3(bucket)
    dest = iota((TILES, TILES), 0)
    lane = iota((TILES, TILES), 1)
    band, lon = dest >> 4, dest & 15
    for r in range(8):
        di, dj = OFFS[r]
        source = (band + di) * LONS + ((lon + dj) & 15)
        shift = as_bf16(lane == source)
        own = (lane >= 96) & (lane < 104) & (dest == lane - 96 + 8 * r)
        if r < 4:
            own = own | ((lane >= 104) & (lane < 112) & (dest == lane - 104 + 64 + 8 * r))
        pick = as_bf16(own)
        total = sum(dot(shift, part) for part in parts) + sum(dot(part, pick) for part in parts)
        send[:, r, :] = total


def centre(record, row_shift, col_shift):
    cell = record[0]
    row = jnp.floor(cell * (1.0 / 128.0))
    col = cell - row * 128.0
    return row + row_shift, col + col_shift


def factor(place, centre_row, offset_row):
    gap = place - centre_row
    distance = gap - offset_row
    return jnp.where(jnp.abs(gap) <= float(REACH), jnp.exp(-(distance * distance) * INV), 0.0)


def places(count, start):
    return (iota((count, 128), 0) + start).astype(F32)


def conv_rows(x_ref, t_ref, base, first, count, length):
    total = None
    for q in range(KERNEL):
        m = base + q
        before = x_ref[m, pl.ds(first - 1, count), 0:length, 128:256]
        here = x_ref[m, pl.ds(first, count), 0:length, :]
        after = x_ref[m, pl.ds(first + 1, count), 0:length, 0:128]
        lhs = jnp.concatenate([before, here, after], axis=2).reshape(count * length, 512)
        part = dot(lhs, t_ref[q])
        total = part if total is None else total + part
    return total


def windows(x_ref, m, first):
    before = x_ref[m, first - 1 : first + 15, 0:128, 128:256]
    here = x_ref[m, first : first + 16, 0:128, :]
    after = x_ref[m, first + 1 : first + 17, 0:128, 0:128]
    return jnp.concatenate([before, here, after], axis=2).reshape(2048, 512)


def shifted(x, by):
    return x if by == 0 else pltpu.roll(x, x.shape[0] - by, 0)


def main_kernel(
    band_ref,
    recv,
    cov,
    wbig,
    sel,
    wg,
    wdec,
    t1,
    t2,
    t3,
    out,
    tr,
    lhs_s,
    rhs_s,
    dens,
    stot,
    lgacc,
    st_t,
    x1,
    x2,
    x3,
    win,
    lat,
    lmat,
    gt1,
    gt2,
    predm,
    outc,
):
    band = band_ref[0]

    for r in range(8):
        tr[r] = recv[:, r, :].T

    def station_slot(r, k):
        if r < 8:
            return tr[r, pl.ds(pl.multiple_of(k * 8, 8), 8), :]
        return tr[k, 96:104, :]

    def target_slot(r, k):
        if r < 8:
            return tr[r, pl.ds(pl.multiple_of(64 + k * 8, 8), 8), :]
        return tr[k, 104:112, :]

    dens[...] = jnp.zeros(dens.shape, F32)
    stot[...] = jnp.zeros(stot.shape, F32)
    for r in (8, 0, 1, 2, 3, 4, 5, 6, 7):
        di, dj = OFFS[r]
        n0, n = {0: (0, 80), -1: (0, 16), 1: (64, 16)}[di]
        m0, m = {0: (0, 144), -1: (0, 16), 1: (128, 16)}[dj]

        def station_step(k, carry, r=r, di=di, dj=dj, n0=n0, n=n, m0=m0, m=m):
            rec = station_slot(r, k)
            row, col = centre((rec[5:6],), 64.0 * di + REACH, 128.0 * dj + REACH)
            down = factor(places(n, n0), row, rec[6:7])
            across = factor(places(m, m0), col, rec[7:8])
            at = pl.ds(pl.multiple_of(k * 128, 128), 128)
            later = pl.ds(pl.multiple_of(k * 128 + 1024, 128), 128)
            hi, lo = split2(across)
            rhs_s[0:m, at] = hi
            rhs_s[0:m, later] = lo
            for v in range(5):
                hi, lo = split2(down * rec[v : v + 1])
                lhs_s[v * n : (v + 1) * n, at] = hi
                lhs_s[v * n : (v + 1) * n, later] = lo
            return carry

        lax.fori_loop(0, 8, station_step, 0)
        left, right = lhs_s[0 : 5 * n, :], rhs_s[0:m, :]
        part = dot(left[:, :1024], right[:, :1024], NT)
        part = part + dot(left[:, 1024:], right[:, :1024], NT)
        part = part + dot(left[:, :1024], right[:, 1024:], NT)
        e_row = iota((n, m), 0) + (n0 - REACH - 64 * di)
        e_col = iota((n, m), 1) + (m0 - REACH - 128 * dj)
        inside = (e_row >= 0) & (e_row < 64) & (e_col >= 0) & (e_col < 128)
        for v in range(5):
            piece = part[v * n : (v + 1) * n]
            dens[v, n0 : n0 + n, m0 : m0 + m] += jnp.where(inside, piece, rounded(piece))

    for r in (8, 0, 1, 2, 3, 4, 5, 6, 7):
        di, dj = OFFS[r]
        n0, n = {0: (0, 80), -1: (0, 16), 1: (64, 16)}[di]
        m0, m = {0: (0, 256), -1: (0, 128), 1: (128, 128)}[dj]

        def target_step(k, carry, r=r, di=di, dj=dj, n0=n0, n=n, m0=m0, m=m):
            rec = target_slot(r, k)
            row, col = centre((rec[2:3],), 64.0 * di + REACH, 128.0 * dj + REACH)
            down = factor(places(n, n0), row, rec[3:4])
            across = factor(places(m, m0), col, rec[4:5])
            at = pl.ds(pl.multiple_of(k * 128, 128), 128)
            rhs_s[0:m, at] = across.astype(BF16)
            for v in range(2):
                for p, part in enumerate(split3(down * rec[v : v + 1])):
                    place = pl.ds(pl.multiple_of(k * 128 + 512 * p, 128), 128)
                    lhs_s[v * n : (v + 1) * n, place] = part
            return carry

        lax.fori_loop(0, 4, target_step, 0)
        right = rhs_s[0:m, 0:512]
        spread = sum(dot(lhs_s[0 : 2 * n, 512 * p : 512 * p + 512], right, NT) for p in range(3))
        for v in range(2):
            stot[v, n0 : n0 + n, m0 : m0 + m] += spread[v * n : (v + 1) * n]
        blocks = {0: range(9), -1: (0,), 1: (8,)}[di]
        rows_kept = 144 if dj == 0 else 16
        e_row = (iota((rows_kept, 512), 1) >> 6) - REACH - 64 * di
        e_col = iota((rows_kept, 512), 0) + (m0 - REACH - 128 * dj)
        for block in blocks:
            low = 8 * block - n0
            s8 = jnp.concatenate([spread[v * n + low : v * n + low + 8] for v in range(2)], axis=0)
            hi = rounded(s8)
            mid = rounded(s8 - hi)
            rest = rounded(s8 - hi - mid)
            zero = jnp.zeros_like(s8)
            stack = jnp.concatenate([hi, hi, hi, mid, mid, rest, zero, zero], axis=0)
            left = stack.T[0:rows_kept].astype(BF16)
            piece = dot(left, wg[...])
            row_here = e_row + 8 * block
            inside = (row_here >= 0) & (row_here < 64) & (e_col >= 0) & (e_col < 128)
            piece = jnp.where(inside, piece, rounded(piece))
            if r == 8:
                lgacc[block] = piece
            else:
                lgacc[block, m0 : m0 + rows_kept, :] += piece

    for block in range(9):
        grow = band * 64 + 8 * block - REACH + (iota((144, 512), 1) >> 6)
        grad = rounded(jnp.where((grow >= 0) & (grow < 512), lgacc[block], 0.0))
        for q in range(KERNEL):
            moved = shifted(grad, q + 2)[0:128].astype(BF16)
            x3[q, 2 * block] = moved[:, 0:256]
            x3[q, 2 * block + 1] = moved[:, 256:512]

    x1[:, 0] = jnp.zeros((7, 144, 256), BF16)
    x1[:, 19] = jnp.zeros((7, 144, 256), BF16)

    def lift_step(block, carry):
        rows = pl.ds(pl.multiple_of(block * 8, 8), 8)
        grow = band * 64 + 8 * block - REACH + iota((8, 256), 0)
        real = (grow >= 0) & (grow < 512)
        first = dens[0, rows, :]
        below = jnp.maximum(first, 1.0)
        planes = [first] + [dens[v, rows, :] / below for v in range(1, 5)]
        planes = [rounded(x) for x in planes] + [cov[v, rows, :] for v in range(8)]
        planes = [jnp.where(real, x, 0.0) for x in planes]
        planes = planes + [jnp.zeros((8, 256), F32)] * 3
        left = jnp.concatenate(planes, axis=0).T[0:144].astype(BF16)
        st_t[block] = left
        lifted = rounded(dot(left, wbig[...]))
        for m in range(7):
            moved = shifted(lifted, m).astype(BF16)
            x1[m, 2 * block + 1] = moved[:, 0:256]
            x1[m, 2 * block + 2] = moved[:, 256:512]
        return carry

    lax.fori_loop(0, 9, lift_step, 0)

    def window_step(m, carry):
        left = jnp.concatenate([st_t[m], st_t[m + 1]], axis=1)
        both = dot(left, sel[...])
        for q in range(KERNEL):
            moved = shifted(both, q + 2)[0:128].astype(BF16)
            win[q, 2 * m] = moved[:, 0:128]
            win[q, 2 * m + 1] = moved[:, 128:256]
        return carry

    lax.fori_loop(0, 8, window_step, 0)

    def hidden_step(c, carry):
        value = jnp.maximum(conv_rows(x1, t1, 0, 3 * c + 1, 3, 144), 0.0)
        for i in range(3):
            sr = 3 * c + i
            gone = ((sr == 0) & (band == 0)) | ((sr == 17) & (band == BANDS - 1))
            row = rounded(jnp.where(gone, 0.0, value[144 * i : 144 * i + 144]))
            for q in range(KERNEL):
                x2[q, sr] = shifted(row, q)[0:128].astype(BF16)
        return carry

    lax.fori_loop(0, 6, hidden_step, 0)

    def latent_step(c, carry):
        value = conv_rows(x2, t2, 0, 4 * c + 1, 4, 128)
        own = x1[4, pl.ds(4 * c + 2, 4), 0:128, :].reshape(512, 256)
        latent = (own.astype(F32) + value).astype(BF16)
        lat[pl.ds(4 * c, 4)] = latent.reshape(4, 128, 256)
        outs = dot(wdec[...], latent, NT)
        outs = outs[0:8] + outs[8:16] + outs[16:24]
        for i in range(4):
            lmat[pl.ds(pl.multiple_of(32 * c + 8 * i, 8), 8), :] = outs[:, 128 * i : 128 * i + 128]
        return carry

    lax.fori_loop(0, 4, latent_step, 0)

    grad_out = jnp.zeros((48, 512), F32)
    for m in range(8):
        s8 = jnp.concatenate(
            [pltpu.roll(stot[v, 4 + 8 * m : 12 + 8 * m, :], 252, 1)[:, 0:128] for v in range(2)],
            axis=0,
        )
        left = jnp.concatenate([p.astype(F32) for p in split3(s8)], axis=0).astype(BF16)
        grad_out = grad_out + dot(left, jnp.concatenate([lat[2 * m], lat[2 * m + 1]], axis=1))
    grad_out = grad_out[0:16] + grad_out[16:32] + grad_out[32:48]
    grad_out = jnp.where((iota((16, 512), 0) & 7) == (iota((16, 512), 1) >> 6), grad_out, 0.0)
    grad_out = sum(grad_out[:, 128 * i : 128 * i + 128] for i in range(4))
    grad_out = grad_out + pltpu.roll(grad_out, 64, 1)
    grad_out = jnp.concatenate(
        [jnp.sum(grad_out[8 * v : 8 * v + 8], axis=0, keepdims=True) for v in range(2)], axis=0
    )

    predm[...] = jnp.zeros(predm.shape, F32)
    l_parts = split3(lmat[...])
    for r in range(9):
        di, dj = OFFS[r]
        lo, count = {0: (0, 128), -1: (0, 8), 1: (120, 8)}[di]
        n_iota = iota((count, 128), 0) + lo
        i_row = (4 * (n_iota >> 3) + (n_iota & 3)).astype(F32)
        pieces = [p[lo : lo + count] if count == 128 else None for p in l_parts]
        if count == 8:
            few = lmat[lo : lo + 8, :]
            pieces = [p for p in split3(jnp.concatenate([few, jnp.zeros_like(few)], axis=0))]

        def decode_step(k, carry, r=r, di=di, dj=dj, count=count, i_row=i_row, pieces=pieces):
            rec = target_slot(r, k)
            row, col = centre((rec[2:3],), 64.0 * di, 128.0 * dj)
            across = factor(places(128, 0), col, rec[4:5]).astype(BF16)
            down = factor(i_row, row, rec[3:4])
            mixed = sum(dot(p, across) for p in pieces)[0:count]
            mixed = mixed * down
            eight = jnp.sum(mixed.reshape(count // 8, 8, 128), axis=0)
            for v in range(2):
                line = jnp.sum(eight[4 * v : 4 * v + 4], axis=0, keepdims=True)
                predm[pl.ds(8 * r + 2 * k + v, 1), :] = line
            return carry

        lax.fori_loop(0, 4, decode_step, 0)
    out[:, 13, :] = predm[...].T

    for i in range(16):
        gt1[:, 128 * i : 128 * i + 128] = x3[2, i + 1].astype(F32).T.astype(BF16)

    def store_grad(group, q, corr):
        even = corr[0:64, 0:384] + corr[128:192, 128:512]
        odd = corr[64:128, 0:384] + corr[192:256, 128:512]
        if q % 2 == 0:
            line = even + pltpu.roll(odd, 384 - 64, 1)
        else:
            line = pltpu.roll(even, 64, 1) + odd
        return line

    def all_grads(group, gt, x_ref, base, first):
        lines = []
        for q in range(KERNEL):
            lines.append(store_grad(group, q, dot(gt[...], windows(x_ref, base + q, first))))
        low = iota((64, 128), 1) < 64
        at = pl.ds(64 * group, 64)
        tiles = [lines[0][:, 0:128], lines[0][:, 128:256]]
        tiles.append(jnp.where(low, lines[0][:, 256:384], lines[1][:, 0:128]))
        tiles += [lines[1][:, 128:256], lines[1][:, 256:384]]
        tiles += [lines[2][:, 0:128], lines[2][:, 128:256]]
        tiles.append(jnp.where(low, lines[2][:, 256:384], lines[3][:, 0:128]))
        tiles += [lines[3][:, 128:256], lines[3][:, 256:384]]
        tiles += [lines[4][:, 0:128], lines[4][:, 128:256]]
        tiles.append(jnp.where(low, lines[4][:, 256:384], 0.0))
        for t, tile in enumerate(tiles):
            out[at, t, :] = tile

    all_grads(1, gt1, x2, 0, 1)

    def hidden_grad_step(c, carry):
        value = conv_rows(x3, t3, 0, 4 * c + 1, 4, 128)
        for i in range(4):
            alive = x2[2, 4 * c + i + 1].astype(F32) > 0.0
            row = rounded(jnp.where(alive, value[128 * i : 128 * i + 128], 0.0))
            gt2[:, pl.ds(pl.multiple_of(512 * c + 128 * i, 128), 128)] = row.T.astype(BF16)
        return carry

    lax.fori_loop(0, 4, hidden_grad_step, 0)
    all_grads(0, gt2, x1, 2, 2)

    grad_lift = jnp.zeros((512, 128), F32)
    for q in range(KERNEL):
        corr = dot(gt2[...], win[q].reshape(2048, 128))
        for part in split3(corr):
            grad_lift = grad_lift + dot(t1[q], part)
    same = (iota((512, 128), 0) >> 6) == (iota((512, 128), 1) >> 4)
    grad_lift = jnp.where(same, grad_lift, 0.0)
    direct = dot(gt1[...], win[2].reshape(2048, 128))
    same = (iota((256, 128), 0) >> 6) + 2 == (iota((256, 128), 1) >> 4)
    direct = jnp.where(same, direct, 0.0)
    total = sum(grad_lift[64 * w : 64 * w + 64] for w in range(8))
    total = total + sum(direct[64 * w : 64 * w + 64] for w in range(4))
    for by in (64, 32, 16):
        total = total + pltpu.roll(total, by, 1)
    out[0:64, 14, :] = total
    out[64:128, 14, :] = jnp.concatenate([grad_out, jnp.zeros((62, 128), F32)], axis=0)
    out[:, 15, :] = jnp.zeros((128, 128), F32)


def sum_kernel(recv, tg_tile, tg_rank, perm, back, pred):
    total = jnp.sum(recv[...], axis=0)
    turned = jnp.concatenate([total, jnp.zeros((112, 128), F32)], axis=0).T
    lane = iota((64, 1664), 1)
    channel = iota((64, 1664), 0)
    own = (lane >= 25 * channel) & (lane < 25 * channel + 25)
    line = jnp.zeros((1, 1664), F32)
    for half in range(2):
        left = turned[64 * half : 64 * half + 64]
        spread = sum(dot(part, perm[half]) for part in split3(left))
        line = line + jnp.sum(jnp.where(own, spread, 0.0), axis=0, keepdims=True)
    rows = [line[:, 128 * t : 128 * t + 128] for t in range(13)]
    zero = jnp.zeros((1, 128), F32)
    chunk = jnp.concatenate(rows + [zero, total[14:15], zero], axis=0)
    back[...] = jnp.broadcast_to(chunk[None], back.shape)

    answers = recv[:, 13, :].T
    tile = tg_tile[...]
    count = tile.shape[1]
    band, lon = tile >> 4, tile & 15
    place = iota((TILES, count), 0)
    got = jnp.zeros((8, count), F32)
    for r in range(9):
        di, dj = OFFS[r]
        source = (band - di) * LONS + ((lon - dj) & 15)
        pick = as_bf16(place == source)
        parts = jnp.concatenate([p.astype(F32) for p in split3(answers[8 * r : 8 * r + 8])], axis=0)
        found = dot(parts.astype(BF16), pick)
        got = got + (found[0:8] + found[8:16] + found[16:24])
    rank = tg_rank[0:1, :]
    for v in range(2):
        value = jnp.zeros((1, count), F32)
        for k in range(4):
            value = value + jnp.where(rank == float(k), got[2 * k + v : 2 * k + v + 1], 0.0)
        pred[v : v + 1, :] = value


def final_kernel(recv, first, second, lift, outw):
    for t in range(13):
        wide = 128 if t < 12 else 64
        first[:, 128 * t : 128 * t + wide] = recv[0:64, t, 0:wide]
        second[:, 128 * t : 128 * t + wide] = recv[64:128, t, 0:wide]
    turned = recv[:, 14, :].T
    lift[...] = turned[0:13, 0:64]
    outw[...] = turned[0:64, 64:66]


def selection():
    table = np.zeros((2, 16, 8, 2, 8, 16), np.float32)
    for group in range(2):
        for w in range(8):
            at = 4 * group + w + 2
            for k in range(16):
                table[at // 8, k, at % 8, group, w, k] = 1.0
    return table.reshape(256, 256)


def permutation():
    table = np.zeros((2, 128, 1664), np.float32)
    for q in range(5):
        for p in range(5):
            at = q * 5 + p
            for c in range(64):
                table[at % 2, at // 2, c * 25 + p * 5 + q] = 1.0
    return table


def toeplitz(blocks):
    shifts = [
        jnp.pad(blocks, ((0, 0), (ii, 3 - ii), (0, 0), (0, 0))) for ii in range(4)
    ]
    return jnp.stack(shifts, axis=3).reshape(KERNEL, 512, 256)


def parts3(x):
    hi = lax.reduce_precision(x, 8, 7)
    mid = lax.reduce_precision(x - hi, 8, 7)
    return hi, mid, lax.reduce_precision(x - hi - mid, 8, 7)


def ring(axis, step):
    size = lax.axis_size(axis)
    return [(i, (i + step) % size) for i in range(size)]


def call(kernel, outs, scratch=(), specs=None, limit=56):
    return pl.pallas_call(
        kernel,
        out_shape=outs,
        **({} if specs is None else {"in_specs": specs}),
        scratch_shapes=scratch,
        compiler_params=pltpu.CompilerParams(vmem_limit_bytes=limit * 2**20),
    )


def shards(
    station_tile,
    station_cell,
    station_offset,
    station_values,
    covariates,
    target_tile,
    target_cell,
    target_offset,
    lift_weight,
    first_kernel,
    second_kernel,
    out_weight,
    cotangent,
):
    n_s, n_t = station_cell.shape[0], target_cell.shape[0]
    axes = ("lat", "lon")
    st_tile = station_tile.reshape(1, n_s)
    tg_tile = target_tile.reshape(1, n_t)
    st_rec = jnp.concatenate(
        [
            jnp.ones((1, n_s), F32),
            station_values,
            station_cell.astype(F32)[None],
            station_offset,
        ],
        axis=0,
    )
    tg_rec = jnp.concatenate(
        [
            cotangent,
            target_cell.astype(F32)[None],
            target_offset,
            jnp.zeros((3, n_t), F32),
        ],
        axis=0,
    )
    send, tg_rank = call(
        pack_kernel,
        (
            jax.ShapeDtypeStruct((TILES, 8, 128), F32),
            jax.ShapeDtypeStruct((8, n_t), F32),
        ),
    )(st_tile, st_rec, tg_tile, tg_rec)
    recv = lax.all_to_all(send, axes, split_axis=0, concat_axis=0, tiled=True)

    north = lax.ppermute(covariates[:, 60:64, :], "lat", ring("lat", 1))
    south = lax.ppermute(covariates[:, 0:4, :], "lat", ring("lat", -1))
    tall = jnp.concatenate([north, covariates, south], axis=1)
    west = lax.ppermute(tall[:, :, 124:128], "lon", ring("lon", 1))
    east = lax.ppermute(tall[:, :, 0:4], "lon", ring("lon", -1))
    cov = jnp.concatenate([west, tall, east], axis=2)
    cov = jnp.pad(cov.astype(F32), ((0, 0), (0, 0), (0, 120)))

    eye8 = jnp.eye(8, dtype=F32)
    eye4 = jnp.eye(4, dtype=F32)
    lift_pad = jnp.pad(lift_weight.astype(F32), ((0, 3), (0, 0)))
    wbig = (lift_pad[:, None, None, :] * eye8[None, :, :, None]).reshape(128, 512).astype(BF16)
    w_parts = parts3(out_weight)
    w_rows = [
        (p.T[:, None, None, :] * eye8[None, :, :, None]).reshape(16, 512) for p in w_parts
    ]
    blank = jnp.zeros((32, 512), F32)
    wg = jnp.concatenate(
        [w_rows[0], w_rows[1], w_rows[2], w_rows[0], w_rows[1], w_rows[0], blank], axis=0
    ).astype(BF16)
    wdec = jnp.concatenate(
        [(p.T[:, None, None, :] * eye4[None, :, :, None]).reshape(8, 256) for p in w_parts]
        + [jnp.zeros((8, 256), F32)],
        axis=0,
    ).astype(BF16)

    k1 = first_kernel.reshape(64, 64, KERNEL, KERNEL)
    k2 = second_kernel.reshape(64, 64, KERNEL, KERNEL)
    t1 = toeplitz(jnp.transpose(k1, (3, 2, 1, 0)))
    t2 = toeplitz(jnp.transpose(k2, (3, 2, 1, 0)))
    t3 = toeplitz(jnp.transpose(k2, (3, 2, 0, 1))[::-1, ::-1])
    sel = jnp.asarray(selection(), BF16)
    perm = jnp.asarray(permutation(), BF16)
    band = lax.axis_index("lat").astype(jnp.int32).reshape(1)

    vmem = pl.BlockSpec(memory_space=pltpu.VMEM)
    grads = call(
        main_kernel,
        jax.ShapeDtypeStruct((TILES, 16, 128), F32),
        specs=[pl.BlockSpec(memory_space=pltpu.SMEM)] + [vmem] * 9,
        scratch=[
            pltpu.VMEM((8, 128, 128), F32),
            pltpu.VMEM((400, 2048), BF16),
            pltpu.VMEM((256, 2048), BF16),
            pltpu.VMEM((5, 80, 256), F32),
            pltpu.VMEM((2, 80, 256), F32),
            pltpu.VMEM((9, 144, 512), F32),
            pltpu.VMEM((9, 144, 128), BF16),
            pltpu.VMEM((7, 20, 144, 256), BF16),
            pltpu.VMEM((5, 18, 128, 256), BF16),
            pltpu.VMEM((5, 18, 128, 256), BF16),
            pltpu.VMEM((5, 16, 128, 128), BF16),
            pltpu.VMEM((16, 128, 256), BF16),
            pltpu.VMEM((128, 128), F32),
            pltpu.VMEM((256, 2048), BF16),
            pltpu.VMEM((256, 2048), BF16),
            pltpu.VMEM((128, 128), F32),
            pltpu.VMEM((8, 128), F32),
        ],
    )(band, recv, cov, wbig, sel, wg, wdec, t1, t2, t3)

    got = lax.all_to_all(grads, axes, split_axis=0, concat_axis=0, tiled=True)
    back, predictions = call(
        sum_kernel,
        (
            jax.ShapeDtypeStruct((TILES, 16, 128), F32),
            jax.ShapeDtypeStruct((2, n_t), F32),
        ),
    )(got, tg_tile, tg_rank, perm)
    summed = lax.all_to_all(back, axes, split_axis=0, concat_axis=0, tiled=True)
    grad_first, grad_second, grad_lift, grad_out = call(
        final_kernel,
        (
            jax.ShapeDtypeStruct((64, 1600), F32),
            jax.ShapeDtypeStruct((64, 1600), F32),
            jax.ShapeDtypeStruct((13, 64), F32),
            jax.ShapeDtypeStruct((64, 2), F32),
        ),
    )(summed)
    return predictions, grad_lift, grad_first, grad_second, grad_out


def solution(mesh):
    placed = (
        P(("lat", "lon"), None),
        P(("lat", "lon")),
        P(None, ("lat", "lon")),
        P(None, ("lat", "lon")),
        P(None, "lat", "lon"),
        P(("lat", "lon"), None),
        P(("lat", "lon")),
        P(None, ("lat", "lon")),
        P(),
        P(),
        P(),
        P(),
        P(None, ("lat", "lon")),
    )
    return jax.shard_map(
        shards,
        mesh=mesh,
        in_specs=placed,
        out_specs=(P(None, ("lat", "lon")), P(), P(), P(), P()),
        check_vma=False,
    )
```

```python
import jax
import jax.numpy as jnp
import numpy as np
from jax import lax
from jax.experimental import pallas as pl
from jax.experimental.pallas import tpu as pltpu
from jax.sharding import PartitionSpec as P

KERNEL = 5
REACH = 4
INV = 1.0 / 4.5
F32 = jnp.float32
BF16 = jnp.bfloat16
BANDS = 8
LONS = 16
TILES = 128
SIDES = (3, 4)
ENDS = (1, 6)
CORNERS = (0, 2, 5, 7)
OFFS = ((-1, -1), (-1, 0), (-1, 1), (0, -1), (0, 1), (1, -1), (1, 0), (1, 1), (0, 0))
NT = (((1,), (1,)), ((), ()))
NN = (((1,), (0,)), ((), ()))
SIX = ((0, 0), (0, 1), (1, 0), (1, 1), (0, 2), (2, 0))


def dot(a, b, dims=NN):
    return lax.dot_general(a, b, dims, preferred_element_type=F32)


def iota(shape, axis):
    return lax.broadcasted_iota(jnp.int32, shape, axis)


def split2(x):
    hi = x.astype(BF16)
    return hi, (x - hi.astype(F32)).astype(BF16)


def split3(x):
    hi = x.astype(BF16)
    rest = x - hi.astype(F32)
    mid = rest.astype(BF16)
    return hi, mid, (rest - mid.astype(F32)).astype(BF16)


def rounded(x):
    return x.astype(BF16).astype(F32)


def as_bf16(mask):
    return mask.astype(F32).astype(BF16)


def reaches(cell, di, dj, reach):
    row, col = cell >> 7, cell & 127
    near = row >= 0
    if di == -1:
        near = near & (row >= 64 - reach)
    if di == 1:
        near = near & (row < reach)
    if dj == -1:
        near = near & (col >= 128 - reach)
    if dj == 1:
        near = near & (col < reach)
    return near


def ranked(dests):
    count = dests[0].shape[1]
    earlier = as_bf16(iota((count, count), 0) < iota((count, count), 1))
    hits = [iota((TILES, count), 0) == dest for dest in dests]
    hits_b = [as_bf16(h) for h in hits]
    before = dot(jnp.concatenate(hits_b, axis=0), earlier)
    ranks = []
    for i, h in enumerate(hits):
        mine = before[TILES * i : TILES * i + TILES]
        ranks.append(jnp.sum(jnp.where(h, mine, 0.0), axis=0, keepdims=True))
    return hits_b, ranks


def pack_kernel(
    st_tile,
    st_cell,
    st_off,
    st_val,
    tg_tile,
    tg_cell,
    tg_off,
    tg_cot,
    cov,
    send,
    tg_rank,
    to_east,
    to_west,
):
    n_s, n_t = st_tile.shape[1], tg_tile.shape[1]
    s_cell, t_cell = st_cell[...], tg_cell[...]
    s_tile, t_tile = st_tile[...], tg_tile[...]
    s_rec = jnp.concatenate(
        [jnp.ones((1, n_s), F32), st_val[...], s_cell.astype(F32), st_off[...]], axis=0
    )
    t_rec = jnp.concatenate(
        [
            tg_cot[...],
            t_cell.astype(F32),
            tg_off[...],
            jnp.ones((1, n_t), F32),
            jnp.zeros((2, n_t), F32),
        ],
        axis=0,
    )
    s_dests, t_dests = [], []
    for dests, tile, cell, reach in ((s_dests, s_tile, s_cell, 8), (t_dests, t_tile, t_cell, 6)):
        for di, dj in OFFS[:8]:
            to = ((tile >> 4) - di) * LONS + (((tile & 15) - dj) & 15)
            dests.append(jnp.where(reaches(cell, di, dj, reach), to, -1))
        dests.append(tile)
    s_hits, s_ranks = ranked(s_dests)
    t_hits, t_ranks = ranked(t_dests)
    lane = iota((TILES, TILES), 1)

    def slots(r):
        s_rows = [jnp.where(s_ranks[r] == k, s_rec, 0.0) for k in range(8)]
        hi, mid, rest = split3(jnp.concatenate(s_rows, axis=0))
        s_found = dot(s_hits[r], jnp.concatenate([hi, rest, mid], axis=0), NT)
        first = s_found[:, 0:128]
        second = jnp.concatenate([s_found[:, 128:192], jnp.zeros((TILES, 64), F32)], axis=1)
        s_found = first + second + pltpu.roll(first, 64, 1)
        t_rows = [jnp.where(t_ranks[r] == k, t_rec, 0.0) for k in range(4)]
        hi, mid, rest = split3(jnp.concatenate(t_rows, axis=0))
        blank = jnp.zeros((64, n_t), BF16)
        tail = jnp.zeros((32, n_t), BF16)
        parts = jnp.concatenate([blank, hi, rest, blank, mid, tail], axis=0)
        t_found = dot(t_hits[r], parts, NT)
        first = t_found[:, 0:128]
        t_found = first + t_found[:, 128:256] + pltpu.roll(first, 96, 1)
        return jnp.where(lane < 64, s_found, jnp.where(lane < 96, t_found, 0.0))

    parts = split3(slots(8))
    tg_rank[8:16, :] = jnp.broadcast_to(t_ranks[8], (8, n_t))
    dest = iota((TILES, TILES), 0)
    for r in range(8):
        tg_rank[r : r + 1, :] = jnp.where(t_dests[r] < 0, -1.0, t_ranks[r])
        own = (lane >= 96) & (lane < 104) & (dest == lane - 96 + 8 * r)
        if r < 4:
            own = own | ((lane >= 104) & (lane < 112) & (dest == lane - 104 + 64 + 8 * r))
        pick = as_bf16(own)
        send[:, r, :] = slots(r) + sum(dot(part, pick) for part in parts)

    blank = jnp.zeros((64, 128), F32)
    east, west = [], []
    for v in range(8):
        turned = jnp.concatenate([cov[v].astype(F32), blank], axis=0).T
        east.append(turned[120:128])
        west.append(turned[0:8])
    to_east[...] = jnp.concatenate(east, axis=0).astype(BF16)
    to_west[...] = jnp.concatenate(west, axis=0).astype(BF16)

    band, lon = lax.axis_index("lat"), lax.axis_index("lon")
    lane = iota((8, 128), 1)
    for r in CORNERS:
        di, dj = OFFS[r]
        rows = cov[:, 48:64, :] if di < 0 else cov[:, 0:16, :]
        rows = rows.astype(F32)
        block = jnp.zeros((8, 128), F32)
        for i in range(4):
            line = rows[:, 12 + i if di < 0 else i, :]
            to = 112 + 4 * i
            line = pltpu.roll(line, (to - (124 if dj < 0 else 0)) % 128, 1)
            block = jnp.where((lane >= to) & (lane < to + 4), line, block)
        to_band = band - di

        @pl.when((to_band >= 0) & (to_band < BANDS))
        def _(block=block, to_band=to_band, dj=dj):
            dest = to_band * LONS + ((lon - dj) & 15)
            send[pl.ds(dest, 1)] += block[None]


def build_weights(k1, k2, lift_w, out_w, t1, t2, t3, wbig, wg, wdec, kt):
    half = jnp.zeros((128, 64), F32)
    for b in range(13):
        wide = 128 if b < 12 else 64
        piece = jnp.concatenate(
            [k1[:, 128 * b : 128 * b + wide], k2[:, 128 * b : 128 * b + wide]], axis=0
        ).astype(F32)
        if wide == 64:
            piece = jnp.concatenate([piece, half], axis=1)
        kt[128 * b : 128 * b + 128, :] = piece.T
    low = iota((64, 128), 1) < 64
    none = jnp.zeros((64, 128), F32)
    for q in range(KERNEL):
        v = [kt[pl.ds(p * 5 + q, 64, stride=25), :] for p in range(5)]
        turned = [pltpu.roll(x, 64, 1) for x in v]
        for w in range(8):
            rows = slice(64 * w, 64 * w + 64)
            for side, p in enumerate((w, w - 2)):
                lanes = slice(128 * side, 128 * side + 128)
                if p < 0 or p > 5:
                    g1 = g2 = g3 = none
                else:
                    here, before = (v[p], turned[p]) if p < 5 else (none, none), (
                        (v[p - 1], turned[p - 1]) if p > 0 else (none, none)
                    )
                    g1 = jnp.where(low, here[0], before[1])
                    g2 = jnp.where(low, here[1], before[0])
                    pair = jnp.concatenate(
                        [v[4 - p] if p < 5 else none, v[5 - p] if p > 0 else none], axis=0
                    )
                    g3 = pair.T[64:128]
                t1[q, rows, lanes] = g1.astype(BF16)
                t2[q, rows, lanes] = g2.astype(BF16)
                t3[4 - q, rows, lanes] = g3.astype(BF16)
    same = (iota((8, 512), 1) >> 6) == iota((8, 512), 0)
    lift2 = lift_w[...].astype(F32)
    lift2 = jnp.concatenate([lift2, lift2], axis=1)
    rows = []
    for k in range(13):
        row = jnp.concatenate([lift2[k : k + 1, :]] * 4, axis=1)
        rows.append(jnp.where(same, row, 0.0))
    rows += [jnp.zeros((8, 512), F32)] * 3
    wbig[...] = jnp.concatenate(rows, axis=0).astype(BF16)
    out2 = jnp.concatenate([out_w[...], out_w[...]], axis=1)
    parts = [x.astype(F32) for x in split3(out2)]
    blank = jnp.zeros((16, 512), F32)
    rows = []
    for x in parts:
        two = [jnp.concatenate([x[v : v + 1, :]] * 4, axis=1) for v in range(2)]
        rows.append(jnp.concatenate([jnp.where(same, y, 0.0) for y in two], axis=0))
    stack = [rows[0], rows[1], rows[2], rows[0], rows[1], rows[0], blank, blank]
    wg[...] = jnp.concatenate(stack, axis=0).astype(BF16)
    sub = iota((8, 256), 0)
    same = (iota((8, 256), 1) >> 6) == (sub & 3)
    rows = []
    for x in parts:
        two = [jnp.concatenate([x[v : v + 1, :]] * 2, axis=1) for v in range(2)]
        rows.append(jnp.where(same, jnp.where(sub < 4, two[0], two[1]), 0.0))
    wdec[...] = jnp.concatenate(rows + [jnp.zeros((8, 256), F32)], axis=0).astype(BF16)


def centre(cell, row_shift, col_shift):
    row = jnp.floor(cell * (1.0 / 128.0))
    col = cell - row * 128.0
    return row + row_shift, col + col_shift


def factor(place, centre_row, offset_row):
    gap = place - centre_row
    distance = gap - offset_row
    return jnp.where(jnp.abs(gap) <= float(REACH), jnp.exp(-(distance * distance) * INV), 0.0)


def places(count, start):
    return (iota((count, 128), 0) + start).astype(F32)


def repeated(start):
    return ((iota((128, 128), 0) & 15) + start).astype(F32)


def conv_rows(x_ref, t_ref, first, count, length):
    total = None
    for q in range(KERNEL):
        before = x_ref[q, pl.ds(first - 1, count), 0:length, 128:256]
        here = x_ref[q, pl.ds(first, count), 0:length, :]
        after = x_ref[q, pl.ds(first + 1, count), 0:length, 0:128]
        lhs = jnp.concatenate([before, here, after], axis=2).reshape(count * length, 512)
        part = dot(lhs, t_ref[q])
        total = part if total is None else total + part
    return total


def windows(x_ref, q, first):
    before = x_ref[q, first - 1 : first + 15, 0:128, 128:256]
    here = x_ref[q, first : first + 16, 0:128, :]
    after = x_ref[q, first + 1 : first + 17, 0:128, 0:128]
    return jnp.concatenate([before, here, after], axis=2).reshape(2048, 512)


def shifted(x, by):
    return x if by == 0 else pltpu.roll(x, x.shape[0] - by, 0)


def fold_rows(corr, q):
    even = corr[0:64, 0:384] + corr[128:192, 128:512]
    odd = corr[64:128, 0:384] + corr[192:256, 128:512]
    if q % 2 == 0:
        return even + pltpu.roll(odd, 384 - 64, 1)
    return pltpu.roll(even, 64, 1) + odd


def kernel_grad_rows(gt, x_ref, base, first):
    lines = [
        fold_rows(dot(gt[...], windows(x_ref, base + q, first)), q) for q in range(KERNEL)
    ]
    lane = iota((64, 128), 1)
    low = lane < 64
    tiles = [lines[0][:, 0:128], lines[0][:, 128:256]]
    tiles.append(jnp.where(low, lines[0][:, 256:384], lines[1][:, 0:128]))
    tiles += [lines[1][:, 128:256], lines[1][:, 256:384]]
    tiles += [lines[2][:, 0:128], lines[2][:, 128:256]]
    tiles.append(jnp.where(low, lines[2][:, 256:384], lines[3][:, 0:128]))
    tiles += [lines[3][:, 128:256], lines[3][:, 256:384]]
    tiles += [lines[4][:, 0:128], lines[4][:, 128:256]]
    tiles += [jnp.where(low, lines[4][:, 256:384], 0.0), jnp.zeros((64, 128), F32)]
    quarter = (lane & 63) < 32
    rows = []
    for r in range(7):
        a, b = tiles[2 * r], tiles[2 * r + 1]
        rows.append(
            (
                jnp.where(quarter, a, pltpu.roll(b, 32, 1)),
                jnp.where(quarter, pltpu.roll(a, 96, 1), b),
            )
        )
    return rows


def neighbour_count(tr, start, stride_rows, slots):
    most = tr[0, pl.ds(start, slots, stride=8), :]
    for r in range(1, 8):
        most = jnp.maximum(most, tr[r, pl.ds(start, slots, stride=8), :])
    most = jnp.max(most, axis=1, keepdims=True)
    return jnp.sum(most).astype(jnp.int32)


def spans(r):
    di, dj = OFFS[r]
    n0, n = {0: (0, 80), -1: (0, 16), 1: (64, 16)}[di]
    m0, m = {0: (0, 144), -1: (0, 16), 1: (128, 16)}[dj]
    return di, dj, n0, n, m0, m


def inside_tile(shape, row, col):
    return (row >= 0) & (row < 64) & (col >= 0) & (col < 128)


def main_kernel(
    recv,
    cov,
    north,
    south,
    west,
    east,
    k1,
    k2,
    lift_w,
    out_w,
    sel,
    out,
    tr,
    dens,
    stot,
    gt1,
    lhs_s,
    rhs_s,
    side_p,
    end_p,
    corner_p,
    side_s,
    end_s,
    corner_s,
    lgacc,
    covx,
    st_t,
    x1,
    x2,
    x3,
    win,
    lat,
    lmat,
    gt2,
    predm,
    last,
    t1,
    t2,
    t3,
    wbig,
    wg,
    wdec,
    kt,
):
    band, lon = lax.axis_index("lat"), lax.axis_index("lon")
    build_weights(k1, k2, lift_w, out_w, t1, t2, t3, wbig, wg, wdec, kt)

    for r in range(8):
        tr[r] = recv[:, r, :].T
    station_most = neighbour_count(tr, 0, 8, 8)
    target_most = neighbour_count(tr, 69, 8, 4)

    def station_step(k, carry):
        rec = tr[k, 96:104, :]
        row, col = centre(rec[5:6], REACH, REACH)
        down = factor(places(80, 0), row, rec[6:7])
        across = factor(places(144, 0), col, rec[7:8])
        for p, part in enumerate(split3(across)):
            at = pl.ds(pl.multiple_of(k * 128 + 1024 * p, 128), 128)
            rhs_s[0:144, at] = part
        for v in range(5):
            for p, part in enumerate(split3(down * rec[v : v + 1])):
                at = pl.ds(pl.multiple_of(k * 128 + 1024 * p, 128), 128)
                lhs_s[v * 80 : v * 80 + 80, at] = part
        return carry

    lax.fori_loop(0, 8, station_step, 0)
    part = None
    for a, b in SIX:
        one = dot(
            lhs_s[0:400, 1024 * a : 1024 * a + 1024], rhs_s[0:144, 1024 * b : 1024 * b + 1024], NT
        )
        part = one if part is None else part + one
    inside = inside_tile((80, 144), iota((80, 144), 0) - REACH, iota((80, 144), 1) - REACH)
    dens[...] = jnp.zeros(dens.shape, F32)
    for v in range(5):
        piece = part[v * 80 : v * 80 + 80]
        dens[v, :, 0:144] = jnp.where(inside, piece, rounded(piece))

    side_p[...] = jnp.zeros(side_p.shape, F32)
    end_p[...] = jnp.zeros(end_p.shape, F32)
    corner_p[...] = jnp.zeros(corner_p.shape, F32)

    def neighbour_station_step(k, carry):
        for r in range(8):
            di, dj, n0, n, m0, m = spans(r)
            rec = tr[r, pl.ds(pl.multiple_of(k * 8, 8), 8), :]
            row, col = centre(rec[5:6], 64.0 * di + REACH, 128.0 * dj + REACH)
            down = factor(places(n, n0), row, rec[6:7])
            across = split3(factor(places(m, m0), col, rec[7:8]))
            left = split3(jnp.concatenate([down * rec[v : v + 1] for v in range(5)], axis=0))
            left = jnp.concatenate([left[a] for a, _ in SIX], axis=1)
            right = jnp.concatenate([across[b] for _, b in SIX], axis=1)
            more = dot(left, right, NT)
            if r in SIDES:
                side_p[SIDES.index(r), :, 0:16] += more
            elif r in ENDS:
                end_p[ENDS.index(r), :, 0:144] += more
            else:
                corner_p[CORNERS.index(r), :, 0:16] += more
        return carry

    lax.fori_loop(0, station_most, neighbour_station_step, 0)
    for r in range(8):
        di, dj, n0, n, m0, m = spans(r)
        inside = inside_tile(
            (n, m),
            iota((n, m), 0) + (n0 - REACH - 64 * di),
            iota((n, m), 1) + (m0 - REACH - 128 * dj),
        )
        for v in range(5):
            if r in SIDES:
                piece = side_p[SIDES.index(r), v * n : v * n + n, 0:m]
            elif r in ENDS:
                piece = end_p[ENDS.index(r), v * n : v * n + n, 0:m]
            else:
                piece = corner_p[CORNERS.index(r), v * n : v * n + n, 0:m]
            dens[v, n0 : n0 + n, m0 : m0 + m] += jnp.where(inside, piece, rounded(piece))

    for k in range(4):
        rec = tr[k, 104:112, :]
        row, col = centre(rec[2:3], REACH, REACH)
        down = factor(places(80, 0), row, rec[3:4])
        across = factor(places(144, 0), col, rec[4:5])
        rhs_s[0:144, 128 * k : 128 * k + 128] = across.astype(BF16)
        for v in range(2):
            for p, part in enumerate(split3(down * rec[v : v + 1])):
                at = 128 * k + 512 * p
                lhs_s[v * 80 : v * 80 + 80, at : at + 128] = part
    right = rhs_s[0:144, 0:512]
    spread = sum(dot(lhs_s[0:160, 512 * p : 512 * p + 512], right, NT) for p in range(3))
    stot[...] = jnp.zeros(stot.shape, F32)
    for v in range(2):
        stot[v, :, 0:144] = spread[80 * v : 80 * v + 80]

    def gradient_rows(s8):
        hi = rounded(s8)
        mid = rounded(s8 - hi)
        rest = rounded(s8 - hi - mid)
        zero = jnp.zeros_like(s8)
        stack = jnp.concatenate([hi, hi, hi, mid, mid, rest, zero, zero], axis=0)
        return stack.T.astype(BF16)

    e_row = (iota((144, 512), 1) >> 6) - REACH
    e_col = iota((144, 512), 0) - REACH
    for block in range(9):
        rows = pl.ds(8 * block, 8)
        s8 = jnp.concatenate([stot[v, rows, :] for v in range(2)], axis=0)
        piece = dot(gradient_rows(s8)[0:144], wg[...])
        inside = inside_tile((144, 512), e_row + 8 * block, e_col)
        lgacc[block] = jnp.where(inside, piece, rounded(piece))

    side_s[...] = jnp.zeros(side_s.shape, F32)
    end_s[...] = jnp.zeros(end_s.shape, F32)
    corner_s[...] = jnp.zeros(corner_s.shape, F32)

    def neighbour_target_step(k, carry):
        for r in range(8):
            di, dj, n0, n, m0, m = spans(r)
            rec = tr[r, pl.ds(pl.multiple_of(64 + k * 8, 8), 8), :]
            row, col = centre(rec[2:3], 64.0 * di + REACH, 128.0 * dj + REACH)
            down = factor(places(n, n0), row, rec[3:4])
            across = factor(places(m, m0) if dj == 0 else repeated(m0), col, rec[4:5]).astype(BF16)
            left = jnp.concatenate([down * rec[v : v + 1] for v in range(2)], axis=0)
            left = jnp.concatenate(split3(left), axis=1)
            more = dot(left, jnp.concatenate([across] * 3, axis=1), NT)
            if r in SIDES:
                side_s[SIDES.index(r)] += more
            elif r in ENDS:
                end_s[ENDS.index(r), :, 0:144] += more
            else:
                corner_s[CORNERS.index(r)] += more
        return carry

    lax.fori_loop(0, target_most, neighbour_target_step, 0)
    for r in range(8):
        di, dj, n0, n, m0, m = spans(r)
        for v in range(2):
            if r in SIDES:
                piece = side_s[SIDES.index(r), v * n : v * n + n, 0:m]
            elif r in ENDS:
                piece = end_s[ENDS.index(r), v * n : v * n + n, 0:m]
            else:
                piece = corner_s[CORNERS.index(r), v * n : v * n + n, 0:m]
            stot[v, n0 : n0 + n, m0 : m0 + m] += piece

    def add_piece(r, block, m0, piece):
        di, dj = OFFS[r]
        kept = piece.shape[0]
        row = (iota((kept, 512), 1) >> 6) - REACH - 64 * di + 8 * block
        col = iota((kept, 512), 0) + (m0 - REACH - 128 * dj)
        piece = jnp.where(inside_tile((kept, 512), row, col), piece, rounded(piece))
        lgacc[block, m0 : m0 + kept, :] += piece

    for i, r in enumerate(ENDS):
        s8 = jnp.concatenate([end_s[i, v * 16 : v * 16 + 8, :] for v in range(2)], axis=0)
        add_piece(r, 0 if r == 1 else 8, 0, dot(gradient_rows(s8)[0:144], wg[...]))
    group = iota((8, 128), 1) >> 4
    for i, r in enumerate(SIDES):
        s8 = []
        for v in range(2):
            line = jnp.zeros((8, 128), F32)
            for block in range(8):
                at = v * 80 + 8 * block
                line = jnp.where(group == block, side_s[i, at : at + 8, :], line)
            s8.append(line)
        many = dot(gradient_rows(jnp.concatenate(s8, axis=0)), wg[...])
        m0 = 0 if r == 3 else 128
        for block in range(8):
            add_piece(r, block, m0, many[16 * block : 16 * block + 16])
    s8 = []
    for v in range(2):
        line = jnp.zeros((8, 128), F32)
        for i in range(2):
            line = jnp.where(group == i, side_s[i, v * 80 + 64 : v * 80 + 72, :], line)
        for i in range(4):
            line = jnp.where(group == 2 + i, corner_s[i, v * 16 : v * 16 + 8, :], line)
        s8.append(line)
    many = dot(gradient_rows(jnp.concatenate(s8, axis=0)), wg[...])
    for i, (r, block) in enumerate(((3, 8), (4, 8), (0, 0), (2, 0), (5, 8), (7, 8))):
        m0 = 0 if OFFS[r][1] < 0 else 128
        add_piece(r, block, m0, many[16 * i : 16 * i + 16])

    for block in range(9):
        grow = band * 64 + 8 * block - REACH + (iota((144, 512), 1) >> 6)
        grad = rounded(jnp.where((grow >= 0) & (grow < 512), lgacc[block], 0.0))
        for q in range(KERNEL):
            moved = shifted(grad, q + 2)[0:128].astype(BF16)
            x3[q, 2 * block] = moved[:, 0:256]
            x3[q, 2 * block + 1] = moved[:, 256:512]
        own = shifted(grad, REACH)[0:128]
        for side in range(2):
            i = 2 * block + side - 1
            if 0 <= i < 16:
                turned = own[:, 256 * side : 256 * side + 256].T
                gt1[:, 128 * i : 128 * i + 128] = turned.astype(BF16)

    covx[...] = jnp.zeros(covx.shape, F32)
    lane = iota((64, 128), 1)
    from_west = west[...].astype(F32).T
    from_east = east[...].astype(F32).T
    wide = jnp.zeros((64, 128), F32)
    few = jnp.zeros((4, 128), F32)
    for v in range(8):
        rows = jnp.concatenate([cov[v].astype(F32), wide], axis=1)
        rows = pltpu.roll(rows, 4, 1)
        left = pltpu.roll(
            jnp.concatenate([from_west[0:64], wide[:, 0:64]], axis=1), 124 - 8 * v, 1
        )
        right = pltpu.roll(
            jnp.concatenate([from_east[0:64], wide[:, 0:64]], axis=1), (132 - 8 * v) % 128, 1
        )
        covx[v, 4:68, 0:128] = jnp.where(lane < 4, left, rows[:, 0:128])
        right = jnp.where((lane >= 4) & (lane < 8), right, rows[:, 128:256])
        covx[v, 4:68, 128:256] = right
        for at, strip in ((0, north), (68, south)):
            rows = jnp.concatenate([strip[v].astype(F32), few], axis=1)
            covx[v, at : at + 4, :] = pltpu.roll(rows, 4, 1)
    lane = iota((8, 128), 1)
    for r in CORNERS:
        di, dj = OFFS[r]
        from_band = jnp.clip(band + di, 0, BANDS - 1)
        block = recv[from_band * LONS + ((lon + dj) & 15)]
        at, tile = (0, 0) if dj < 0 else (4, 128)
        for i in range(4):
            line = pltpu.roll(block, (at - 112 - 4 * i) % 128, 1)
            line = jnp.where((lane >= at) & (lane < at + 4), line, 0.0)
            covx[:, (0 if di < 0 else 68) + i, tile : tile + 128] += line

    x1[:, 0] = jnp.zeros((7, 144, 256), BF16)
    x1[:, 19] = jnp.zeros((7, 144, 256), BF16)

    def lift_step(block, carry):
        rows = pl.ds(pl.multiple_of(block * 8, 8), 8)
        grow = band * 64 + 8 * block - REACH + iota((8, 256), 0)
        real = (grow >= 0) & (grow < 512)
        first = dens[0, rows, :]
        below = jnp.maximum(first, 1.0)
        planes = [first] + [dens[v, rows, :] / below for v in range(1, 5)]
        planes = [rounded(x) for x in planes] + [covx[v, rows, :] for v in range(8)]
        planes = [jnp.where(real, x, 0.0) for x in planes]
        planes = planes + [jnp.zeros((8, 256), F32)] * 3
        left = jnp.concatenate(planes, axis=0).T[0:144].astype(BF16)
        st_t[block] = left
        lifted = rounded(dot(left, wbig[...]))
        for m in range(7):
            moved = shifted(lifted, m).astype(BF16)
            x1[m, 2 * block + 1] = moved[:, 0:256]
            x1[m, 2 * block + 2] = moved[:, 256:512]
        return carry

    lax.fori_loop(0, 9, lift_step, 0, unroll=9)

    def hidden_step(c, carry):
        value = jnp.maximum(conv_rows(x1, t1, 3 * c + 1, 3, 144), 0.0)
        for i in range(3):
            sr = 3 * c + i
            gone = ((sr == 0) & (band == 0)) | ((sr == 17) & (band == BANDS - 1))
            row = rounded(jnp.where(gone, 0.0, value[144 * i : 144 * i + 144]))
            for q in range(KERNEL):
                x2[q, sr] = shifted(row, q)[0:128].astype(BF16)
        return carry

    lax.fori_loop(0, 6, hidden_step, 0, unroll=6)

    for r, (upper, lower) in enumerate(kernel_grad_rows(gt1, x2, 0, 1)):
        if r == 6:
            last[0:64, :] = upper
            last[64:128, :] = lower
        else:
            lanes = slice(896 + 128 * r, 1024 + 128 * r)
            out[0:64, 0, lanes] = upper
            out[64:128, 0, lanes] = lower

    def latent_step(c, carry):
        value = conv_rows(x2, t2, 4 * c + 1, 4, 128)
        own = x1[4, pl.ds(4 * c + 2, 4), 0:128, :].reshape(512, 256)
        latent = (own.astype(F32) + value).astype(BF16)
        lat[pl.ds(4 * c, 4)] = latent.reshape(4, 128, 256)
        outs = dot(wdec[...], latent, NT)
        outs = outs[0:8] + outs[8:16] + outs[16:24]
        for i in range(4):
            lmat[pl.ds(pl.multiple_of(32 * c + 8 * i, 8), 8), :] = outs[:, 128 * i : 128 * i + 128]
        return carry

    lax.fori_loop(0, 4, latent_step, 0)

    grad_out = jnp.zeros((48, 512), F32)
    for m in range(8):
        s8 = jnp.concatenate(
            [pltpu.roll(stot[v, 4 + 8 * m : 12 + 8 * m, :], 252, 1)[:, 0:128] for v in range(2)],
            axis=0,
        )
        left = jnp.concatenate([p.astype(F32) for p in split3(s8)], axis=0).astype(BF16)
        grad_out = grad_out + dot(left, jnp.concatenate([lat[2 * m], lat[2 * m + 1]], axis=1))
    grad_out = grad_out[0:16] + grad_out[16:32] + grad_out[32:48]
    grad_out = jnp.where((iota((16, 512), 0) & 7) == (iota((16, 512), 1) >> 6), grad_out, 0.0)
    grad_out = sum(grad_out[:, 128 * i : 128 * i + 128] for i in range(4))
    grad_out = grad_out + pltpu.roll(grad_out, 64, 1)
    grad_out = jnp.concatenate(
        [jnp.sum(grad_out[8 * v : 8 * v + 8], axis=0, keepdims=True) for v in range(2)], axis=0
    )

    predm[...] = jnp.zeros(predm.shape, F32)
    n_iota = iota((128, 128), 0)
    i_row = (4 * (n_iota >> 3) + (n_iota & 3)).astype(F32)
    pieces = split3(lmat[...])
    stacked_l = jnp.concatenate(pieces, axis=1)
    pad = jnp.zeros((8, 128), F32)
    ends = []
    for lo in (0, 120):
        few = split3(jnp.concatenate([lmat[lo : lo + 8, :], pad], axis=0))
        ends.append(jnp.concatenate(few, axis=1))

    def decode_line(mixed, down, row):
        mixed = mixed * down
        eight = jnp.sum(mixed.reshape(mixed.shape[0] // 8, 8, 128), axis=0)
        lines = [jnp.sum(eight[4 * v : 4 * v + 4], axis=0, keepdims=True) for v in range(2)]
        for v in range(2):
            predm[pl.ds(row + v, 1), :] = lines[v]

    acrosses, downs = [], []
    for k in range(4):
        rec = tr[k, 104:112, :]
        row, col = centre(rec[2:3], 0.0, 0.0)
        acrosses.append(factor(places(128, 0), col, rec[4:5]).astype(BF16))
        downs.append(factor(i_row, row, rec[3:4]))
    wide = jnp.concatenate(acrosses, axis=1)
    mixed = dot(stacked_l, jnp.concatenate([wide] * 3, axis=0))
    for k in range(4):
        decode_line(mixed[:, 128 * k : 128 * k + 128], downs[k], 64 + 2 * k)

    def decode_step(k, carry):
        for r in range(8):
            di, dj = OFFS[r]
            rec = tr[r, pl.ds(pl.multiple_of(64 + k * 8, 8), 8), :]
            row, col = centre(rec[2:3], 64.0 * di, 128.0 * dj)
            across = factor(places(128, 0), col, rec[4:5]).astype(BF16)
            across = jnp.concatenate([across] * 3, axis=0)
            if di == 0:
                decode_line(dot(stacked_l, across), factor(i_row, row, rec[3:4]), 8 * r + 2 * k)
            else:
                lo = 0 if di < 0 else 120
                few = dot(ends[0 if di < 0 else 1], across)[0:8]
                decode_line(few, factor(i_row[lo : lo + 8], row, rec[3:4]), 8 * r + 2 * k)
        return carry

    lax.fori_loop(0, target_most, decode_step, 0)

    def hidden_grad_step(c, carry):
        value = conv_rows(x3, t3, 4 * c + 1, 4, 128)
        for i in range(4):
            alive = x2[2, 4 * c + i + 1].astype(F32) > 0.0
            row = rounded(jnp.where(alive, value[128 * i : 128 * i + 128], 0.0))
            gt2[:, pl.ds(pl.multiple_of(512 * c + 128 * i, 128), 128)] = row.T.astype(BF16)
        return carry

    lax.fori_loop(0, 4, hidden_grad_step, 0, unroll=4)
    for r, (upper, lower) in enumerate(kernel_grad_rows(gt2, x1, 2, 2)):
        if r == 6:
            answers = pltpu.roll(predm[...].T, 32, 1)
            upper = upper + answers[0:64]
            lower = lower + answers[64:128]
        lanes = slice(128 * r, 128 * r + 128)
        out[0:64, 0, lanes] = upper
        out[64:128, 0, lanes] = lower

    def window_step(m, carry):
        left = jnp.concatenate([st_t[m], st_t[m + 1]], axis=1)
        both = dot(left, sel[...])
        for q in range(KERNEL):
            moved = shifted(both, q + 2)[0:128].astype(BF16)
            win[2 * m, :, 128 * q : 128 * q + 128] = moved[:, 0:128]
            win[2 * m + 1, :, 128 * q : 128 * q + 128] = moved[:, 128:256]
        return carry

    lax.fori_loop(0, 8, window_step, 0, unroll=8)
    corr = dot(gt2[...], win[...].reshape(2048, 640))
    grad_lift = jnp.zeros((512, 256), F32)
    for q in range(KERNEL):
        two = jnp.concatenate(split2(corr[:, 128 * q : 128 * q + 128]), axis=1)
        grad_lift = grad_lift + dot(t1[q], two)
    grad_lift = grad_lift[:, 0:128] + grad_lift[:, 128:256]
    same = (iota((512, 128), 0) >> 6) == (iota((512, 128), 1) >> 4)
    grad_lift = jnp.where(same, grad_lift, 0.0)
    direct = dot(gt1[...], win[:, :, 256:384].reshape(2048, 128))
    same = (iota((256, 128), 0) >> 6) + 2 == (iota((256, 128), 1) >> 4)
    direct = jnp.where(same, direct, 0.0)
    total = sum(grad_lift[64 * w : 64 * w + 64] for w in range(8))
    total = total + sum(direct[64 * w : 64 * w + 64] for w in range(4))
    for by in (64, 32, 16):
        total = total + pltpu.roll(total, by, 1)
    misc = jnp.concatenate([total, grad_out, jnp.zeros((62, 128), F32)], axis=0)
    misc = jnp.where(iota((128, 128), 1) < 64, misc, 0.0)
    out[:, 0, 1664:1792] = last[...] + pltpu.roll(misc, 64, 1)


def summed_chunk(total, perm, shift):
    turned = jnp.concatenate([total, jnp.zeros((120, 128), F32)], axis=0).T
    lane = iota((32, 896), 1)
    channel = iota((32, 896), 0)
    own = (lane >= 25 * channel) & (lane < 25 * channel + 25)
    spread = jnp.zeros((32, 896), F32)
    for g in range(4):
        left = turned[32 * g : 32 * g + 32, 0:16]
        spread = spread + sum(dot(part, perm[g]) for part in split3(left))
    line = jnp.sum(jnp.where(own, spread, 0.0), axis=0, keepdims=True)
    line = jnp.broadcast_to(line, (8, 896))
    line = jnp.where(shift, pltpu.roll(line, 32, 1), line)
    return [line[0:1, 128 * t : 128 * t + 128] for t in range(7)]


def sum_kernel(recv, perm, tg_tile, tg_rank, back, pred):
    total = jnp.sum(recv[...], axis=0)
    lines = [total[:, 128 * t : 128 * t + 128] for t in range(14)]
    zero = jnp.zeros((1, 128), F32)
    shift = lax.axis_index("lat") >= BANDS // 2
    misc = jnp.where(iota((1, 128), 1) < 64, pltpu.roll(lines[13], 64, 1), 0.0)
    high = rounded(misc)
    rows = summed_chunk(jnp.concatenate(lines[0:7] + [zero], axis=0), perm, shift) + [high]
    rows += summed_chunk(jnp.concatenate(lines[7:14] + [zero], axis=0), perm, shift)
    chunk = jnp.concatenate(rows + [misc - high], axis=0).astype(BF16)
    back[...] = jnp.broadcast_to(chunk[None], back.shape)

    answers = recv[:, 0, 768:896].T
    tile = tg_tile[...]
    count = tile.shape[1]
    band, lon = tile >> 4, tile & 15
    place = iota((TILES, count), 0)
    value = [jnp.zeros((1, count), F32) for _ in range(2)]
    for r in range(9):
        di, dj = OFFS[r]
        source = (band - di) * LONS + ((lon - dj) & 15)
        pick = as_bf16(place == source)
        eight = answers[32 + 8 * r : 40 + 8 * r]
        parts = jnp.concatenate([p.astype(F32) for p in split3(eight)], axis=0)
        found = dot(parts.astype(BF16), pick)
        found = found[0:8] + found[8:16] + found[16:24]
        rank = tg_rank[r : r + 1, :]
        for v in range(2):
            for k in range(4):
                line = found[2 * k + v : 2 * k + v + 1]
                value[v] = value[v] + jnp.where(rank == float(k), line, 0.0)
    for v in range(2):
        pred[v : v + 1, :] = value[v]


def final_kernel(recv, first, second, lift, outw, wide_s):
    wide_s[...] = recv[...].astype(F32)
    low = iota((64, 128), 1) < 32
    for base, to in ((0, first), (8, second)):
        for t in range(13):
            if t < 6:
                to[:, 128 * t : 128 * t + 128] = wide_s[0:64, base + t, :]
            elif t == 6:
                to[:, 768:896] = jnp.where(
                    low, wide_s[0:64, base + 6, :], wide_s[64:128, base, :]
                )
            else:
                wide = 128 if t < 12 else 64
                to[:, 128 * t : 128 * t + wide] = wide_s[64:128, base + t - 6, 0:wide]
    turned = (wide_s[:, 7, :] + wide_s[:, 15, :]).T
    lift[...] = turned[0:13, 0:64]
    outw[...] = (wide_s[64:72, 7, 0:64] + wide_s[64:72, 15, 0:64])[0:2]


def selection():
    table = np.zeros((2, 16, 8, 2, 8, 16), np.float32)
    for group in range(2):
        for w in range(8):
            at = 4 * group + w + 2
            for k in range(16):
                table[at // 8, k, at % 8, group, w, k] = 1.0
    return table.reshape(256, 256)


def permutation():
    table = np.zeros((4, 16, 896), np.float32)
    for g in range(4):
        for r in range(7):
            at = 4 * r + (g >> 1) + 2 * (g & 1)
            if at < 25:
                q, p = at // 5, at % 5
                for c in range(32):
                    table[g, r, c * 25 + p * 5 + q] = 1.0
    return table


def ring(axis, step):
    size = lax.axis_size(axis)
    return [(i, (i + step) % size) for i in range(size)]


def shape(*dims, dtype=F32):
    return jax.ShapeDtypeStruct(dims, dtype)


def call(kernel, outs, scratch=(), limit=60):
    return pl.pallas_call(
        kernel,
        out_shape=outs,
        scratch_shapes=scratch,
        compiler_params=pltpu.CompilerParams(vmem_limit_bytes=limit * 2**20),
    )


def shards(
    station_tile,
    station_cell,
    station_offset,
    station_values,
    covariates,
    target_tile,
    target_cell,
    target_offset,
    lift_weight,
    first_kernel,
    second_kernel,
    out_weight,
    cotangent,
):
    n_s, n_t = station_cell.shape[0], target_cell.shape[0]
    axes = ("lat", "lon")
    tg_tile = target_tile.reshape(1, n_t)
    send, tg_rank, to_east, to_west = call(
        pack_kernel,
        (
            shape(TILES, 8, 128),
            shape(16, n_t),
            shape(64, 128, dtype=BF16),
            shape(64, 128, dtype=BF16),
        ),
    )(
        station_tile.reshape(1, n_s),
        station_cell.reshape(1, n_s),
        station_offset,
        station_values,
        tg_tile,
        target_cell.reshape(1, n_t),
        target_offset,
        cotangent,
        covariates,
    )
    recv = lax.all_to_all(send, axes, split_axis=0, concat_axis=0, tiled=True)

    north = lax.ppermute(covariates[:, 60:64, :], "lat", ring("lat", 1))
    south = lax.ppermute(covariates[:, 0:4, :], "lat", ring("lat", -1))
    west = lax.ppermute(to_east, "lon", ring("lon", 1))
    east = lax.ppermute(to_west, "lon", ring("lon", -1))

    sel = jnp.asarray(selection(), BF16)
    perm = jnp.asarray(permutation(), BF16)
    grads = call(
        main_kernel,
        shape(TILES, 1, 1792),
        scratch=[
            pltpu.VMEM((8, 128, 128), F32),
            pltpu.VMEM((5, 80, 256), F32),
            pltpu.VMEM((2, 80, 256), F32),
            pltpu.VMEM((256, 2048), BF16),
            pltpu.VMEM((400, 3072), BF16),
            pltpu.VMEM((144, 3072), BF16),
            pltpu.VMEM((2, 400, 128), F32),
            pltpu.VMEM((2, 80, 256), F32),
            pltpu.VMEM((4, 80, 128), F32),
            pltpu.VMEM((2, 160, 128), F32),
            pltpu.VMEM((2, 32, 256), F32),
            pltpu.VMEM((4, 32, 128), F32),
            pltpu.VMEM((9, 144, 512), F32),
            pltpu.VMEM((8, 72, 256), F32),
            pltpu.VMEM((9, 144, 128), BF16),
            pltpu.VMEM((7, 20, 144, 256), BF16),
            pltpu.VMEM((5, 18, 128, 256), BF16),
            pltpu.VMEM((5, 18, 128, 256), BF16),
            pltpu.VMEM((16, 128, 640), BF16),
            pltpu.VMEM((16, 128, 256), BF16),
            pltpu.VMEM((128, 128), F32),
            pltpu.VMEM((256, 2048), BF16),
            pltpu.VMEM((128, 128), F32),
            pltpu.VMEM((128, 128), F32),
            pltpu.VMEM((5, 512, 256), BF16),
            pltpu.VMEM((5, 512, 256), BF16),
            pltpu.VMEM((5, 512, 256), BF16),
            pltpu.VMEM((128, 512), BF16),
            pltpu.VMEM((128, 512), BF16),
            pltpu.VMEM((32, 256), BF16),
            pltpu.VMEM((1664, 128), F32),
        ],
        limit=52,
    )(recv, covariates, north, south, west, east, first_kernel, second_kernel, lift_weight, out_weight.T, sel)
    got = lax.all_to_all(grads, axes, split_axis=0, concat_axis=0, tiled=True)
    back, predictions = call(
        sum_kernel,
        (shape(TILES, 16, 128, dtype=BF16), shape(2, n_t)),
        limit=24,
    )(got, perm, tg_tile, tg_rank)
    summed = lax.all_to_all(back, axes, split_axis=0, concat_axis=0, tiled=True)
    grad_first, grad_second, grad_lift, grad_out = call(
        final_kernel,
        (shape(64, 1600), shape(64, 1600), shape(13, 64), shape(2, 64)),
        scratch=[pltpu.VMEM((TILES, 16, 128), F32)],
        limit=24,
    )(summed)
    return predictions, grad_lift, grad_first, grad_second, grad_out.T


def solution(mesh):
    placed = (
        P(("lat", "lon"), None),
        P(("lat", "lon")),
        P(None, ("lat", "lon")),
        P(None, ("lat", "lon")),
        P(None, "lat", "lon"),
        P(("lat", "lon"), None),
        P(("lat", "lon")),
        P(None, ("lat", "lon")),
        P(),
        P(),
        P(),
        P(),
        P(None, ("lat", "lon")),
    )
    return jax.shard_map(
        shards,
        mesh=mesh,
        in_specs=placed,
        out_specs=(P(None, ("lat", "lon")), P(), P(), P(), P()),
        check_vma=False,
    )
```

```python
import jax
import jax.numpy as jnp
import numpy as np
from jax import lax
from jax.experimental import pallas as pl
from jax.experimental.pallas import tpu as pltpu
from jax.sharding import PartitionSpec as P

KERNEL = 5
REACH = 4
INV = 1.0 / 4.5
F32 = jnp.float32
BF16 = jnp.bfloat16
BANDS = 8
LONS = 16
TILES = 128
SIDES = (3, 4)
ENDS = (1, 6)
CORNERS = (0, 2, 5, 7)
OFFS = ((-1, -1), (-1, 0), (-1, 1), (0, -1), (0, 1), (1, -1), (1, 0), (1, 1), (0, 0))
NT = (((1,), (1,)), ((), ()))
NN = (((1,), (0,)), ((), ()))
SIX = ((0, 0), (0, 1), (1, 0), (1, 1), (0, 2), (2, 0))


def dot(a, b, dims=NN):
    return lax.dot_general(a, b, dims, preferred_element_type=F32)


def iota(shape, axis):
    return lax.broadcasted_iota(jnp.int32, shape, axis)


def split2(x):
    hi = x.astype(BF16)
    return hi, (x - hi.astype(F32)).astype(BF16)


def split3(x):
    hi = x.astype(BF16)
    rest = x - hi.astype(F32)
    mid = rest.astype(BF16)
    return hi, mid, (rest - mid.astype(F32)).astype(BF16)


def rounded(x):
    return x.astype(BF16).astype(F32)


def as_bf16(mask):
    return mask.astype(F32).astype(BF16)


def reaches(cell, di, dj, reach):
    row, col = cell >> 7, cell & 127
    near = row >= 0
    if di == -1:
        near = near & (row >= 64 - reach)
    if di == 1:
        near = near & (row < reach)
    if dj == -1:
        near = near & (col >= 128 - reach)
    if dj == 1:
        near = near & (col < reach)
    return near


def ranked(dests):
    count = dests[0].shape[1]
    earlier = as_bf16(iota((count, count), 0) < iota((count, count), 1))
    hits = [iota((TILES, count), 0) == dest for dest in dests]
    hits_b = [as_bf16(h) for h in hits]
    before = dot(jnp.concatenate(hits_b, axis=0), earlier)
    ranks = []
    for i, h in enumerate(hits):
        mine = before[TILES * i : TILES * i + TILES]
        ranks.append(jnp.sum(jnp.where(h, mine, 0.0), axis=0, keepdims=True))
    return hits_b, ranks


def pack_kernel(
    st_tile,
    st_cell,
    st_off,
    st_val,
    tg_tile,
    tg_cell,
    tg_off,
    tg_cot,
    cov,
    send,
    tg_rank,
    to_east,
    to_west,
):
    n_s, n_t = st_tile.shape[1], tg_tile.shape[1]
    s_cell, t_cell = st_cell[...], tg_cell[...]
    s_tile, t_tile = st_tile[...], tg_tile[...]
    s_rec = jnp.concatenate(
        [jnp.ones((1, n_s), F32), st_val[...], s_cell.astype(F32), st_off[...]], axis=0
    )
    t_rec = jnp.concatenate(
        [
            tg_cot[...],
            t_cell.astype(F32),
            tg_off[...],
            jnp.ones((1, n_t), F32),
            jnp.zeros((2, n_t), F32),
        ],
        axis=0,
    )
    s_dests, t_dests = [], []
    for dests, tile, cell, reach in ((s_dests, s_tile, s_cell, 8), (t_dests, t_tile, t_cell, 6)):
        for di, dj in OFFS[:8]:
            to = ((tile >> 4) - di) * LONS + (((tile & 15) - dj) & 15)
            dests.append(jnp.where(reaches(cell, di, dj, reach), to, -1))
        dests.append(tile)
    s_hits, s_ranks = ranked(s_dests)
    t_hits, t_ranks = ranked(t_dests)
    lane = iota((TILES, TILES), 1)

    def slots(r):
        s_rows = [jnp.where(s_ranks[r] == k, s_rec, 0.0) for k in range(8)]
        hi, mid, rest = split3(jnp.concatenate(s_rows, axis=0))
        s_found = dot(s_hits[r], jnp.concatenate([hi, rest, mid], axis=0), NT)
        first = s_found[:, 0:128]
        second = jnp.concatenate([s_found[:, 128:192], jnp.zeros((TILES, 64), F32)], axis=1)
        s_found = first + second + pltpu.roll(first, 64, 1)
        t_rows = [jnp.where(t_ranks[r] == k, t_rec, 0.0) for k in range(4)]
        hi, mid, rest = split3(jnp.concatenate(t_rows, axis=0))
        blank = jnp.zeros((64, n_t), BF16)
        tail = jnp.zeros((32, n_t), BF16)
        parts = jnp.concatenate([blank, hi, rest, blank, mid, tail], axis=0)
        t_found = dot(t_hits[r], parts, NT)
        first = t_found[:, 0:128]
        t_found = first + t_found[:, 128:256] + pltpu.roll(first, 96, 1)
        return jnp.where(lane < 64, s_found, jnp.where(lane < 96, t_found, 0.0))

    parts = split3(slots(8))
    tg_rank[8:16, :] = jnp.broadcast_to(t_ranks[8], (8, n_t))
    dest = iota((TILES, TILES), 0)
    for r in range(8):
        tg_rank[r : r + 1, :] = jnp.where(t_dests[r] < 0, -1.0, t_ranks[r])
        own = (lane >= 96) & (lane < 104) & (dest == lane - 96 + 8 * r)
        if r < 4:
            own = own | ((lane >= 104) & (lane < 112) & (dest == lane - 104 + 64 + 8 * r))
        pick = as_bf16(own)
        send[:, r, :] = slots(r) + sum(dot(part, pick) for part in parts)

    blank = jnp.zeros((64, 128), F32)
    east, west = [], []
    for v in range(8):
        turned = jnp.concatenate([cov[v].astype(F32), blank], axis=0).T
        east.append(turned[120:128])
        west.append(turned[0:8])
    to_east[...] = jnp.concatenate(east, axis=0).astype(BF16)
    to_west[...] = jnp.concatenate(west, axis=0).astype(BF16)

    band, lon = lax.axis_index("lat"), lax.axis_index("lon")
    lane = iota((8, 128), 1)
    for r in CORNERS:
        di, dj = OFFS[r]
        rows = cov[:, 48:64, :] if di < 0 else cov[:, 0:16, :]
        rows = rows.astype(F32)
        block = jnp.zeros((8, 128), F32)
        for i in range(4):
            line = rows[:, 12 + i if di < 0 else i, :]
            to = 112 + 4 * i
            line = pltpu.roll(line, (to - (124 if dj < 0 else 0)) % 128, 1)
            block = jnp.where((lane >= to) & (lane < to + 4), line, block)
        to_band = band - di

        @pl.when((to_band >= 0) & (to_band < BANDS))
        def _(block=block, to_band=to_band, dj=dj):
            dest = to_band * LONS + ((lon - dj) & 15)
            send[pl.ds(dest, 1)] += block[None]


def build_weights(k1, k2, lift_w, out_w, t1, t2, t3, wbig, wg, wdec, kt):
    half = jnp.zeros((128, 64), F32)
    for b in range(13):
        wide = 128 if b < 12 else 64
        piece = jnp.concatenate(
            [k1[:, 128 * b : 128 * b + wide], k2[:, 128 * b : 128 * b + wide]], axis=0
        ).astype(F32)
        if wide == 64:
            piece = jnp.concatenate([piece, half], axis=1)
        kt[128 * b : 128 * b + 128, :] = piece.T
    low = iota((64, 128), 1) < 64
    none = jnp.zeros((64, 128), F32)
    for q in range(KERNEL):
        v = [kt[pl.ds(p * 5 + q, 64, stride=25), :] for p in range(5)]
        turned = [pltpu.roll(x, 64, 1) for x in v]
        for w in range(8):
            rows = slice(64 * w, 64 * w + 64)
            for side, p in enumerate((w, w - 2)):
                lanes = slice(128 * side, 128 * side + 128)
                if p < 0 or p > 5:
                    g1 = g2 = g3 = none
                else:
                    here, before = (v[p], turned[p]) if p < 5 else (none, none), (
                        (v[p - 1], turned[p - 1]) if p > 0 else (none, none)
                    )
                    g1 = jnp.where(low, here[0], before[1])
                    g2 = jnp.where(low, here[1], before[0])
                    pair = jnp.concatenate(
                        [v[4 - p] if p < 5 else none, v[5 - p] if p > 0 else none], axis=0
                    )
                    g3 = pair.T[64:128]
                t1[q, rows, lanes] = g1.astype(BF16)
                t2[q, rows, lanes] = g2.astype(BF16)
                t3[4 - q, rows, lanes] = g3.astype(BF16)
    same = (iota((8, 512), 1) >> 6) == iota((8, 512), 0)
    lift2 = lift_w[...].astype(F32)
    lift2 = jnp.concatenate([lift2, lift2], axis=1)
    rows = []
    for k in range(13):
        row = jnp.concatenate([lift2[k : k + 1, :]] * 4, axis=1)
        rows.append(jnp.where(same, row, 0.0))
    rows += [jnp.zeros((8, 512), F32)] * 3
    wbig[...] = jnp.concatenate(rows, axis=0).astype(BF16)
    out2 = jnp.concatenate([out_w[...], out_w[...]], axis=1)
    parts = [x.astype(F32) for x in split3(out2)]
    blank = jnp.zeros((16, 512), F32)
    rows = []
    for x in parts:
        two = [jnp.concatenate([x[v : v + 1, :]] * 4, axis=1) for v in range(2)]
        rows.append(jnp.concatenate([jnp.where(same, y, 0.0) for y in two], axis=0))
    stack = [rows[0], rows[1], rows[2], rows[0], rows[1], rows[0], blank, blank]
    wg[...] = jnp.concatenate(stack, axis=0).astype(BF16)
    sub = iota((8, 256), 0)
    same = (iota((8, 256), 1) >> 6) == (sub & 3)
    rows = []
    for x in parts:
        two = [jnp.concatenate([x[v : v + 1, :]] * 2, axis=1) for v in range(2)]
        rows.append(jnp.where(same, jnp.where(sub < 4, two[0], two[1]), 0.0))
    wdec[...] = jnp.concatenate(rows + [jnp.zeros((8, 256), F32)], axis=0).astype(BF16)


def centre(cell, row_shift, col_shift):
    row = jnp.floor(cell * (1.0 / 128.0))
    col = cell - row * 128.0
    return row + row_shift, col + col_shift


def factor(place, centre_row, offset_row):
    gap = place - centre_row
    distance = gap - offset_row
    return jnp.where(jnp.abs(gap) <= float(REACH), jnp.exp(-(distance * distance) * INV), 0.0)


def places(count, start):
    return (iota((count, 128), 0) + start).astype(F32)


def repeated(start):
    return ((iota((128, 128), 0) & 15) + start).astype(F32)


def conv_rows(x_ref, t_ref, first, count, length):
    total = None
    for q in range(KERNEL):
        before = x_ref[q, pl.ds(first - 1, count), 0:length, 128:256]
        here = x_ref[q, pl.ds(first, count), 0:length, :]
        after = x_ref[q, pl.ds(first + 1, count), 0:length, 0:128]
        lhs = jnp.concatenate([before, here, after], axis=2).reshape(count * length, 512)
        part = dot(lhs, t_ref[q])
        total = part if total is None else total + part
    return total


def windows(x_ref, q, first):
    before = x_ref[q, first - 1 : first + 15, 0:128, 128:256]
    here = x_ref[q, first : first + 16, 0:128, :]
    after = x_ref[q, first + 1 : first + 17, 0:128, 0:128]
    return jnp.concatenate([before, here, after], axis=2).reshape(2048, 512)


def shifted(x, by):
    return x if by == 0 else pltpu.roll(x, x.shape[0] - by, 0)


def fold_rows(corr, q):
    even = corr[0:64, 0:384] + corr[128:192, 128:512]
    odd = corr[64:128, 0:384] + corr[192:256, 128:512]
    if q % 2 == 0:
        return even + pltpu.roll(odd, 384 - 64, 1)
    return pltpu.roll(even, 64, 1) + odd


def kernel_grad_rows(gt, x_ref, base, first):
    lines = [
        fold_rows(dot(gt[...], windows(x_ref, base + q, first)), q) for q in range(KERNEL)
    ]
    lane = iota((64, 128), 1)
    low = lane < 64
    tiles = [lines[0][:, 0:128], lines[0][:, 128:256]]
    tiles.append(jnp.where(low, lines[0][:, 256:384], lines[1][:, 0:128]))
    tiles += [lines[1][:, 128:256], lines[1][:, 256:384]]
    tiles += [lines[2][:, 0:128], lines[2][:, 128:256]]
    tiles.append(jnp.where(low, lines[2][:, 256:384], lines[3][:, 0:128]))
    tiles += [lines[3][:, 128:256], lines[3][:, 256:384]]
    tiles += [lines[4][:, 0:128], lines[4][:, 128:256]]
    tiles += [jnp.where(low, lines[4][:, 256:384], 0.0), jnp.zeros((64, 128), F32)]
    quarter = (lane & 63) < 32
    rows = []
    for r in range(7):
        a, b = tiles[2 * r], tiles[2 * r + 1]
        rows.append(
            (
                jnp.where(quarter, a, pltpu.roll(b, 32, 1)),
                jnp.where(quarter, pltpu.roll(a, 96, 1), b),
            )
        )
    return rows


def neighbour_count(tr, start, stride_rows, slots):
    most = tr[0, pl.ds(start, slots, stride=8), :]
    for r in range(1, 8):
        most = jnp.maximum(most, tr[r, pl.ds(start, slots, stride=8), :])
    most = jnp.max(most, axis=1, keepdims=True)
    return jnp.sum(most).astype(jnp.int32)


def spans(r):
    di, dj = OFFS[r]
    n0, n = {0: (0, 80), -1: (0, 16), 1: (64, 16)}[di]
    m0, m = {0: (0, 144), -1: (0, 16), 1: (128, 16)}[dj]
    return di, dj, n0, n, m0, m


def inside_tile(shape, row, col):
    return (row >= 0) & (row < 64) & (col >= 0) & (col < 128)


def main_kernel(
    recv,
    cov,
    north,
    south,
    west,
    east,
    k1,
    k2,
    lift_w,
    out_w,
    sel,
    out,
    tr,
    dens,
    stot,
    gt1,
    lhs_s,
    rhs_s,
    side_p,
    end_p,
    corner_p,
    side_s,
    end_s,
    corner_s,
    lgacc,
    covx,
    st_t,
    x1,
    x2,
    x3,
    win,
    lat,
    lmat,
    gt2,
    predm,
    last,
    t1,
    t2,
    t3,
    wbig,
    wg,
    wdec,
    kt,
):
    band, lon = lax.axis_index("lat"), lax.axis_index("lon")
    build_weights(k1, k2, lift_w, out_w, t1, t2, t3, wbig, wg, wdec, kt)

    for r in range(8):
        tr[r] = recv[:, r, :].T
    station_most = neighbour_count(tr, 0, 8, 8)
    target_most = neighbour_count(tr, 69, 8, 4)

    def station_step(k, carry):
        rec = tr[k, 96:104, :]
        row, col = centre(rec[5:6], REACH, REACH)
        down = factor(places(80, 0), row, rec[6:7])
        across = factor(places(144, 0), col, rec[7:8])
        for p, part in enumerate(split3(across)):
            at = pl.ds(pl.multiple_of(k * 128 + 1024 * p, 128), 128)
            rhs_s[0:144, at] = part
        for v in range(5):
            for p, part in enumerate(split3(down * rec[v : v + 1])):
                at = pl.ds(pl.multiple_of(k * 128 + 1024 * p, 128), 128)
                lhs_s[v * 80 : v * 80 + 80, at] = part
        return carry

    lax.fori_loop(0, 8, station_step, 0)
    part = None
    for a, b in SIX:
        one = dot(
            lhs_s[0:400, 1024 * a : 1024 * a + 1024], rhs_s[0:144, 1024 * b : 1024 * b + 1024], NT
        )
        part = one if part is None else part + one
    inside = inside_tile((80, 144), iota((80, 144), 0) - REACH, iota((80, 144), 1) - REACH)
    dens[...] = jnp.zeros(dens.shape, F32)
    for v in range(5):
        piece = part[v * 80 : v * 80 + 80]
        dens[v, :, 0:144] = jnp.where(inside, piece, rounded(piece))

    side_p[...] = jnp.zeros(side_p.shape, F32)
    end_p[...] = jnp.zeros(end_p.shape, F32)
    corner_p[...] = jnp.zeros(corner_p.shape, F32)

    def neighbour_station_step(k, carry):
        for r in range(8):
            di, dj, n0, n, m0, m = spans(r)
            rec = tr[r, pl.ds(pl.multiple_of(k * 8, 8), 8), :]
            row, col = centre(rec[5:6], 64.0 * di + REACH, 128.0 * dj + REACH)
            down = factor(places(n, n0), row, rec[6:7])
            across = split3(factor(places(m, m0), col, rec[7:8]))
            left = split3(jnp.concatenate([down * rec[v : v + 1] for v in range(5)], axis=0))
            left = jnp.concatenate([left[a] for a, _ in SIX], axis=1)
            right = jnp.concatenate([across[b] for _, b in SIX], axis=1)
            more = dot(left, right, NT)
            if r in SIDES:
                side_p[SIDES.index(r), :, 0:16] += more
            elif r in ENDS:
                end_p[ENDS.index(r), :, 0:144] += more
            else:
                corner_p[CORNERS.index(r), :, 0:16] += more
        return carry

    lax.fori_loop(0, station_most, neighbour_station_step, 0)
    for r in range(8):
        di, dj, n0, n, m0, m = spans(r)
        inside = inside_tile(
            (n, m),
            iota((n, m), 0) + (n0 - REACH - 64 * di),
            iota((n, m), 1) + (m0 - REACH - 128 * dj),
        )
        for v in range(5):
            if r in SIDES:
                piece = side_p[SIDES.index(r), v * n : v * n + n, 0:m]
            elif r in ENDS:
                piece = end_p[ENDS.index(r), v * n : v * n + n, 0:m]
            else:
                piece = corner_p[CORNERS.index(r), v * n : v * n + n, 0:m]
            dens[v, n0 : n0 + n, m0 : m0 + m] += jnp.where(inside, piece, rounded(piece))

    for k in range(4):
        rec = tr[k, 104:112, :]
        row, col = centre(rec[2:3], REACH, REACH)
        down = factor(places(80, 0), row, rec[3:4])
        across = factor(places(144, 0), col, rec[4:5])
        rhs_s[0:144, 128 * k : 128 * k + 128] = across.astype(BF16)
        for v in range(2):
            for p, part in enumerate(split3(down * rec[v : v + 1])):
                at = 128 * k + 512 * p
                lhs_s[v * 80 : v * 80 + 80, at : at + 128] = part
    right = rhs_s[0:144, 0:512]
    spread = sum(dot(lhs_s[0:160, 512 * p : 512 * p + 512], right, NT) for p in range(3))
    stot[...] = jnp.zeros(stot.shape, F32)
    for v in range(2):
        stot[v, :, 0:144] = spread[80 * v : 80 * v + 80]

    def gradient_rows(s8):
        hi = rounded(s8)
        mid = rounded(s8 - hi)
        rest = rounded(s8 - hi - mid)
        zero = jnp.zeros_like(s8)
        stack = jnp.concatenate([hi, hi, hi, mid, mid, rest, zero, zero], axis=0)
        return stack.T.astype(BF16)

    e_row = (iota((144, 512), 1) >> 6) - REACH
    e_col = iota((144, 512), 0) - REACH
    for block in range(9):
        rows = pl.ds(8 * block, 8)
        s8 = jnp.concatenate([stot[v, rows, :] for v in range(2)], axis=0)
        piece = dot(gradient_rows(s8)[0:144], wg[...])
        inside = inside_tile((144, 512), e_row + 8 * block, e_col)
        lgacc[block] = jnp.where(inside, piece, rounded(piece))

    side_s[...] = jnp.zeros(side_s.shape, F32)
    end_s[...] = jnp.zeros(end_s.shape, F32)
    corner_s[...] = jnp.zeros(corner_s.shape, F32)

    def neighbour_target_step(k, carry):
        for r in range(8):
            di, dj, n0, n, m0, m = spans(r)
            rec = tr[r, pl.ds(pl.multiple_of(64 + k * 8, 8), 8), :]
            row, col = centre(rec[2:3], 64.0 * di + REACH, 128.0 * dj + REACH)
            down = factor(places(n, n0), row, rec[3:4])
            across = factor(places(m, m0) if dj == 0 else repeated(m0), col, rec[4:5]).astype(BF16)
            left = jnp.concatenate([down * rec[v : v + 1] for v in range(2)], axis=0)
            left = jnp.concatenate(split3(left), axis=1)
            more = dot(left, jnp.concatenate([across] * 3, axis=1), NT)
            if r in SIDES:
                side_s[SIDES.index(r)] += more
            elif r in ENDS:
                end_s[ENDS.index(r), :, 0:144] += more
            else:
                corner_s[CORNERS.index(r)] += more
        return carry

    lax.fori_loop(0, target_most, neighbour_target_step, 0)
    for r in range(8):
        di, dj, n0, n, m0, m = spans(r)
        for v in range(2):
            if r in SIDES:
                piece = side_s[SIDES.index(r), v * n : v * n + n, 0:m]
            elif r in ENDS:
                piece = end_s[ENDS.index(r), v * n : v * n + n, 0:m]
            else:
                piece = corner_s[CORNERS.index(r), v * n : v * n + n, 0:m]
            stot[v, n0 : n0 + n, m0 : m0 + m] += piece

    def add_piece(r, block, m0, piece):
        di, dj = OFFS[r]
        kept = piece.shape[0]
        row = (iota((kept, 512), 1) >> 6) - REACH - 64 * di + 8 * block
        col = iota((kept, 512), 0) + (m0 - REACH - 128 * dj)
        piece = jnp.where(inside_tile((kept, 512), row, col), piece, rounded(piece))
        lgacc[block, m0 : m0 + kept, :] += piece

    for i, r in enumerate(ENDS):
        s8 = jnp.concatenate([end_s[i, v * 16 : v * 16 + 8, :] for v in range(2)], axis=0)
        add_piece(r, 0 if r == 1 else 8, 0, dot(gradient_rows(s8)[0:144], wg[...]))
    group = iota((8, 128), 1) >> 4
    for i, r in enumerate(SIDES):
        s8 = []
        for v in range(2):
            line = jnp.zeros((8, 128), F32)
            for block in range(8):
                at = v * 80 + 8 * block
                line = jnp.where(group == block, side_s[i, at : at + 8, :], line)
            s8.append(line)
        many = dot(gradient_rows(jnp.concatenate(s8, axis=0)), wg[...])
        m0 = 0 if r == 3 else 128
        for block in range(8):
            add_piece(r, block, m0, many[16 * block : 16 * block + 16])
    s8 = []
    for v in range(2):
        line = jnp.zeros((8, 128), F32)
        for i in range(2):
            line = jnp.where(group == i, side_s[i, v * 80 + 64 : v * 80 + 72, :], line)
        for i in range(4):
            line = jnp.where(group == 2 + i, corner_s[i, v * 16 : v * 16 + 8, :], line)
        s8.append(line)
    many = dot(gradient_rows(jnp.concatenate(s8, axis=0)), wg[...])
    for i, (r, block) in enumerate(((3, 8), (4, 8), (0, 0), (2, 0), (5, 8), (7, 8))):
        m0 = 0 if OFFS[r][1] < 0 else 128
        add_piece(r, block, m0, many[16 * i : 16 * i + 16])

    for block in range(9):
        grow = band * 64 + 8 * block - REACH + (iota((144, 512), 1) >> 6)
        grad = rounded(jnp.where((grow >= 0) & (grow < 512), lgacc[block], 0.0))
        for q in range(KERNEL):
            moved = shifted(grad, q + 2)[0:128].astype(BF16)
            x3[q, 2 * block] = moved[:, 0:256]
            x3[q, 2 * block + 1] = moved[:, 256:512]
        own = shifted(grad, REACH)[0:128]
        for side in range(2):
            i = 2 * block + side - 1
            if 0 <= i < 16:
                turned = own[:, 256 * side : 256 * side + 256].T
                gt1[:, 128 * i : 128 * i + 128] = turned.astype(BF16)

    covx[...] = jnp.zeros(covx.shape, F32)
    lane = iota((64, 128), 1)
    from_west = west[...].astype(F32).T
    from_east = east[...].astype(F32).T
    wide = jnp.zeros((64, 128), F32)
    few = jnp.zeros((4, 128), F32)
    for v in range(8):
        rows = jnp.concatenate([cov[v].astype(F32), wide], axis=1)
        rows = pltpu.roll(rows, 4, 1)
        left = pltpu.roll(
            jnp.concatenate([from_west[0:64], wide[:, 0:64]], axis=1), 124 - 8 * v, 1
        )
        right = pltpu.roll(
            jnp.concatenate([from_east[0:64], wide[:, 0:64]], axis=1), (132 - 8 * v) % 128, 1
        )
        covx[v, 4:68, 0:128] = jnp.where(lane < 4, left, rows[:, 0:128])
        right = jnp.where((lane >= 4) & (lane < 8), right, rows[:, 128:256])
        covx[v, 4:68, 128:256] = right
        for at, strip in ((0, north), (68, south)):
            rows = jnp.concatenate([strip[v].astype(F32), few], axis=1)
            covx[v, at : at + 4, :] = pltpu.roll(rows, 4, 1)
    lane = iota((8, 128), 1)
    for r in CORNERS:
        di, dj = OFFS[r]
        from_band = jnp.clip(band + di, 0, BANDS - 1)
        block = recv[from_band * LONS + ((lon + dj) & 15)]
        at, tile = (0, 0) if dj < 0 else (4, 128)
        for i in range(4):
            line = pltpu.roll(block, (at - 112 - 4 * i) % 128, 1)
            line = jnp.where((lane >= at) & (lane < at + 4), line, 0.0)
            covx[:, (0 if di < 0 else 68) + i, tile : tile + 128] += line

    x1[:, 0] = jnp.zeros((7, 144, 256), BF16)
    x1[:, 19] = jnp.zeros((7, 144, 256), BF16)

    def lift_step(block, carry):
        rows = pl.ds(pl.multiple_of(block * 8, 8), 8)
        grow = band * 64 + 8 * block - REACH + iota((8, 256), 0)
        real = (grow >= 0) & (grow < 512)
        first = dens[0, rows, :]
        below = jnp.maximum(first, 1.0)
        planes = [first] + [dens[v, rows, :] / below for v in range(1, 5)]
        planes = [rounded(x) for x in planes] + [covx[v, rows, :] for v in range(8)]
        planes = [jnp.where(real, x, 0.0) for x in planes]
        planes = planes + [jnp.zeros((8, 256), F32)] * 3
        left = jnp.concatenate(planes, axis=0).T[0:144].astype(BF16)
        st_t[block] = left
        lifted = rounded(dot(left, wbig[...]))
        for m in range(7):
            moved = shifted(lifted, m).astype(BF16)
            x1[m, 2 * block + 1] = moved[:, 0:256]
            x1[m, 2 * block + 2] = moved[:, 256:512]
        return carry

    lax.fori_loop(0, 9, lift_step, 0, unroll=9)

    def hidden_step(c, carry):
        value = jnp.maximum(conv_rows(x1, t1, 3 * c + 1, 3, 144), 0.0)
        for i in range(3):
            sr = 3 * c + i
            gone = ((sr == 0) & (band == 0)) | ((sr == 17) & (band == BANDS - 1))
            row = rounded(jnp.where(gone, 0.0, value[144 * i : 144 * i + 144]))
            for q in range(KERNEL):
                x2[q, sr] = shifted(row, q)[0:128].astype(BF16)
        return carry

    lax.fori_loop(0, 6, hidden_step, 0, unroll=6)

    for r, (upper, lower) in enumerate(kernel_grad_rows(gt1, x2, 0, 1)):
        if r == 6:
            last[0:64, :] = upper
            last[64:128, :] = lower
        else:
            lanes = slice(896 + 128 * r, 1024 + 128 * r)
            out[0:64, 0, lanes] = upper
            out[64:128, 0, lanes] = lower

    def latent_step(c, carry):
        value = conv_rows(x2, t2, 4 * c + 1, 4, 128)
        own = x1[4, pl.ds(4 * c + 2, 4), 0:128, :].reshape(512, 256)
        latent = (own.astype(F32) + value).astype(BF16)
        lat[pl.ds(4 * c, 4)] = latent.reshape(4, 128, 256)
        return carry

    lax.fori_loop(0, 4, latent_step, 0)
    outs = dot(wdec[...], lat[...].reshape(2048, 256), NT)
    outs = outs[0:8] + outs[8:16] + outs[16:24]
    for i in range(16):
        lmat[8 * i : 8 * i + 8, :] = outs[:, 128 * i : 128 * i + 128]

    grad_out = jnp.zeros((48, 512), F32)
    for m in range(8):
        s8 = jnp.concatenate(
            [pltpu.roll(stot[v, 4 + 8 * m : 12 + 8 * m, :], 252, 1)[:, 0:128] for v in range(2)],
            axis=0,
        )
        left = jnp.concatenate([p.astype(F32) for p in split3(s8)], axis=0).astype(BF16)
        grad_out = grad_out + dot(left, jnp.concatenate([lat[2 * m], lat[2 * m + 1]], axis=1))
    grad_out = grad_out[0:16] + grad_out[16:32] + grad_out[32:48]
    grad_out = jnp.where((iota((16, 512), 0) & 7) == (iota((16, 512), 1) >> 6), grad_out, 0.0)
    grad_out = sum(grad_out[:, 128 * i : 128 * i + 128] for i in range(4))
    grad_out = grad_out + pltpu.roll(grad_out, 64, 1)
    grad_out = jnp.concatenate(
        [jnp.sum(grad_out[8 * v : 8 * v + 8], axis=0, keepdims=True) for v in range(2)], axis=0
    )

    predm[...] = jnp.zeros(predm.shape, F32)
    n_iota = iota((128, 128), 0)
    i_row = (4 * (n_iota >> 3) + (n_iota & 3)).astype(F32)
    pieces = split3(lmat[...])
    stacked_l = jnp.concatenate(pieces, axis=1)
    pad = jnp.zeros((8, 128), F32)
    ends = []
    for lo in (0, 120):
        few = split3(jnp.concatenate([lmat[lo : lo + 8, :], pad], axis=0))
        ends.append(jnp.concatenate(few, axis=1))

    def decode_line(mixed, down, row):
        mixed = mixed * down
        eight = jnp.sum(mixed.reshape(mixed.shape[0] // 8, 8, 128), axis=0)
        lines = [jnp.sum(eight[4 * v : 4 * v + 4], axis=0, keepdims=True) for v in range(2)]
        for v in range(2):
            predm[pl.ds(row + v, 1), :] = lines[v]

    acrosses, downs = [], []
    for k in range(4):
        rec = tr[k, 104:112, :]
        row, col = centre(rec[2:3], 0.0, 0.0)
        acrosses.append(factor(places(128, 0), col, rec[4:5]).astype(BF16))
        downs.append(factor(i_row, row, rec[3:4]))
    wide = jnp.concatenate(acrosses, axis=1)
    mixed = dot(stacked_l, jnp.concatenate([wide] * 3, axis=0))
    for k in range(4):
        decode_line(mixed[:, 128 * k : 128 * k + 128], downs[k], 64 + 2 * k)

    def decode_step(k, carry):
        for r in range(8):
            di, dj = OFFS[r]
            rec = tr[r, pl.ds(pl.multiple_of(64 + k * 8, 8), 8), :]
            row, col = centre(rec[2:3], 64.0 * di, 128.0 * dj)
            across = factor(places(128, 0), col, rec[4:5]).astype(BF16)
            across = jnp.concatenate([across] * 3, axis=0)
            if di == 0:
                decode_line(dot(stacked_l, across), factor(i_row, row, rec[3:4]), 8 * r + 2 * k)
            else:
                lo = 0 if di < 0 else 120
                few = dot(ends[0 if di < 0 else 1], across)[0:8]
                decode_line(few, factor(i_row[lo : lo + 8], row, rec[3:4]), 8 * r + 2 * k)
        return carry

    lax.fori_loop(0, target_most, decode_step, 0)

    def hidden_grad_step(c, carry):
        value = conv_rows(x3, t3, 4 * c + 1, 4, 128)
        for i in range(4):
            alive = x2[2, 4 * c + i + 1].astype(F32) > 0.0
            row = rounded(jnp.where(alive, value[128 * i : 128 * i + 128], 0.0))
            gt2[:, pl.ds(pl.multiple_of(512 * c + 128 * i, 128), 128)] = row.T.astype(BF16)
        return carry

    lax.fori_loop(0, 4, hidden_grad_step, 0, unroll=4)
    for r, (upper, lower) in enumerate(kernel_grad_rows(gt2, x1, 2, 2)):
        if r == 6:
            answers = pltpu.roll(predm[...].T, 32, 1)
            upper = upper + answers[0:64]
            lower = lower + answers[64:128]
        lanes = slice(128 * r, 128 * r + 128)
        out[0:64, 0, lanes] = upper
        out[64:128, 0, lanes] = lower

    def window_step(m, carry):
        left = jnp.concatenate([st_t[m], st_t[m + 1]], axis=1)
        both = dot(left, sel[...])
        for q in range(KERNEL):
            moved = shifted(both, q + 2)[0:128].astype(BF16)
            win[2 * m, :, 128 * q : 128 * q + 128] = moved[:, 0:128]
            win[2 * m + 1, :, 128 * q : 128 * q + 128] = moved[:, 128:256]
        return carry

    lax.fori_loop(0, 8, window_step, 0, unroll=8)
    corr = dot(gt2[...], win[...].reshape(2048, 640))
    grad_lift = jnp.zeros((512, 256), F32)
    for q in range(KERNEL):
        two = jnp.concatenate(split2(corr[:, 128 * q : 128 * q + 128]), axis=1)
        grad_lift = grad_lift + dot(t1[q], two)
    grad_lift = grad_lift[:, 0:128] + grad_lift[:, 128:256]
    same = (iota((512, 128), 0) >> 6) == (iota((512, 128), 1) >> 4)
    grad_lift = jnp.where(same, grad_lift, 0.0)
    direct = dot(gt1[...], win[:, :, 256:384].reshape(2048, 128))
    same = (iota((256, 128), 0) >> 6) + 2 == (iota((256, 128), 1) >> 4)
    direct = jnp.where(same, direct, 0.0)
    total = sum(grad_lift[64 * w : 64 * w + 64] for w in range(8))
    total = total + sum(direct[64 * w : 64 * w + 64] for w in range(4))
    for by in (64, 32, 16):
        total = total + pltpu.roll(total, by, 1)
    misc = jnp.concatenate([total, grad_out, jnp.zeros((62, 128), F32)], axis=0)
    misc = jnp.where(iota((128, 128), 1) < 64, misc, 0.0)
    out[:, 0, 1664:1792] = last[...] + pltpu.roll(misc, 64, 1)


def summed_chunk(total, perm, shift):
    turned = jnp.concatenate([total, jnp.zeros((120, 128), F32)], axis=0).T
    lane = iota((32, 896), 1)
    channel = iota((32, 896), 0)
    own = (lane >= 25 * channel) & (lane < 25 * channel + 25)
    spread = jnp.zeros((32, 896), F32)
    for g in range(4):
        left = turned[32 * g : 32 * g + 32, 0:16]
        spread = spread + sum(dot(part, perm[g]) for part in split3(left))
    line = jnp.sum(jnp.where(own, spread, 0.0), axis=0, keepdims=True)
    line = jnp.broadcast_to(line, (8, 896))
    line = jnp.where(shift, pltpu.roll(line, 32, 1), line)
    return [line[0:1, 128 * t : 128 * t + 128] for t in range(7)]


def sum_kernel(recv, perm, tg_tile, tg_rank, back, pred):
    total = jnp.sum(recv[...], axis=0)
    lines = [total[:, 128 * t : 128 * t + 128] for t in range(14)]
    zero = jnp.zeros((1, 128), F32)
    shift = lax.axis_index("lat") >= BANDS // 2
    misc = jnp.where(iota((1, 128), 1) < 64, pltpu.roll(lines[13], 64, 1), 0.0)
    high = rounded(misc)
    rows = summed_chunk(jnp.concatenate(lines[0:7] + [zero], axis=0), perm, shift) + [high]
    rows += summed_chunk(jnp.concatenate(lines[7:14] + [zero], axis=0), perm, shift)
    chunk = jnp.concatenate(rows + [misc - high], axis=0).astype(BF16)
    back[...] = jnp.broadcast_to(chunk[None], back.shape)

    answers = recv[:, 0, 768:896].T
    tile = tg_tile[...]
    count = tile.shape[1]
    band, lon = tile >> 4, tile & 15
    place = iota((TILES, count), 0)
    value = [jnp.zeros((1, count), F32) for _ in range(2)]
    for r in range(9):
        di, dj = OFFS[r]
        source = (band - di) * LONS + ((lon - dj) & 15)
        pick = as_bf16(place == source)
        eight = answers[32 + 8 * r : 40 + 8 * r]
        parts = jnp.concatenate([p.astype(F32) for p in split3(eight)], axis=0)
        found = dot(parts.astype(BF16), pick)
        found = found[0:8] + found[8:16] + found[16:24]
        rank = tg_rank[r : r + 1, :]
        for v in range(2):
            for k in range(4):
                line = found[2 * k + v : 2 * k + v + 1]
                value[v] = value[v] + jnp.where(rank == float(k), line, 0.0)
    for v in range(2):
        pred[v : v + 1, :] = value[v]


def final_kernel(recv, first, second, lift, outw, wide_s):
    wide_s[...] = recv[...].astype(F32)
    low = iota((64, 128), 1) < 32
    for base, to in ((0, first), (8, second)):
        for t in range(13):
            if t < 6:
                to[:, 128 * t : 128 * t + 128] = wide_s[0:64, base + t, :]
            elif t == 6:
                to[:, 768:896] = jnp.where(
                    low, wide_s[0:64, base + 6, :], wide_s[64:128, base, :]
                )
            else:
                wide = 128 if t < 12 else 64
                to[:, 128 * t : 128 * t + wide] = wide_s[64:128, base + t - 6, 0:wide]
    turned = (wide_s[:, 7, :] + wide_s[:, 15, :]).T
    lift[...] = turned[0:13, 0:64]
    outw[...] = (wide_s[64:72, 7, 0:64] + wide_s[64:72, 15, 0:64])[0:2]


def selection():
    table = np.zeros((2, 16, 8, 2, 8, 16), np.float32)
    for group in range(2):
        for w in range(8):
            at = 4 * group + w + 2
            for k in range(16):
                table[at // 8, k, at % 8, group, w, k] = 1.0
    return table.reshape(256, 256)


def permutation():
    table = np.zeros((4, 16, 896), np.float32)
    for g in range(4):
        for r in range(7):
            at = 4 * r + (g >> 1) + 2 * (g & 1)
            if at < 25:
                q, p = at // 5, at % 5
                for c in range(32):
                    table[g, r, c * 25 + p * 5 + q] = 1.0
    return table


def ring(axis, step):
    size = lax.axis_size(axis)
    return [(i, (i + step) % size) for i in range(size)]


def shape(*dims, dtype=F32):
    return jax.ShapeDtypeStruct(dims, dtype)


def call(kernel, outs, scratch=(), limit=60):
    return pl.pallas_call(
        kernel,
        out_shape=outs,
        scratch_shapes=scratch,
        compiler_params=pltpu.CompilerParams(vmem_limit_bytes=limit * 2**20),
    )


def shards(
    station_tile,
    station_cell,
    station_offset,
    station_values,
    covariates,
    target_tile,
    target_cell,
    target_offset,
    lift_weight,
    first_kernel,
    second_kernel,
    out_weight,
    cotangent,
):
    n_s, n_t = station_cell.shape[0], target_cell.shape[0]
    axes = ("lat", "lon")
    tg_tile = target_tile.reshape(1, n_t)
    send, tg_rank, to_east, to_west = call(
        pack_kernel,
        (
            shape(TILES, 8, 128),
            shape(16, n_t),
            shape(64, 128, dtype=BF16),
            shape(64, 128, dtype=BF16),
        ),
    )(
        station_tile.reshape(1, n_s),
        station_cell.reshape(1, n_s),
        station_offset,
        station_values,
        tg_tile,
        target_cell.reshape(1, n_t),
        target_offset,
        cotangent,
        covariates,
    )
    recv = lax.all_to_all(send, axes, split_axis=0, concat_axis=0, tiled=True)

    north = lax.ppermute(covariates[:, 60:64, :], "lat", ring("lat", 1))
    south = lax.ppermute(covariates[:, 0:4, :], "lat", ring("lat", -1))
    west = lax.ppermute(to_east, "lon", ring("lon", 1))
    east = lax.ppermute(to_west, "lon", ring("lon", -1))

    sel = jnp.asarray(selection(), BF16)
    perm = jnp.asarray(permutation(), BF16)
    grads = call(
        main_kernel,
        shape(TILES, 1, 1792),
        scratch=[
            pltpu.VMEM((8, 128, 128), F32),
            pltpu.VMEM((5, 80, 256), F32),
            pltpu.VMEM((2, 80, 256), F32),
            pltpu.VMEM((256, 2048), BF16),
            pltpu.VMEM((400, 3072), BF16),
            pltpu.VMEM((144, 3072), BF16),
            pltpu.VMEM((2, 400, 128), F32),
            pltpu.VMEM((2, 80, 256), F32),
            pltpu.VMEM((4, 80, 128), F32),
            pltpu.VMEM((2, 160, 128), F32),
            pltpu.VMEM((2, 32, 256), F32),
            pltpu.VMEM((4, 32, 128), F32),
            pltpu.VMEM((9, 144, 512), F32),
            pltpu.VMEM((8, 72, 256), F32),
            pltpu.VMEM((9, 144, 128), BF16),
            pltpu.VMEM((7, 20, 144, 256), BF16),
            pltpu.VMEM((5, 18, 128, 256), BF16),
            pltpu.VMEM((5, 18, 128, 256), BF16),
            pltpu.VMEM((16, 128, 640), BF16),
            pltpu.VMEM((16, 128, 256), BF16),
            pltpu.VMEM((128, 128), F32),
            pltpu.VMEM((256, 2048), BF16),
            pltpu.VMEM((128, 128), F32),
            pltpu.VMEM((128, 128), F32),
            pltpu.VMEM((5, 512, 256), BF16),
            pltpu.VMEM((5, 512, 256), BF16),
            pltpu.VMEM((5, 512, 256), BF16),
            pltpu.VMEM((128, 512), BF16),
            pltpu.VMEM((128, 512), BF16),
            pltpu.VMEM((32, 256), BF16),
            pltpu.VMEM((1664, 128), F32),
        ],
        limit=52,
    )(recv, covariates, north, south, west, east, first_kernel, second_kernel, lift_weight, out_weight.T, sel)
    got = lax.all_to_all(grads, axes, split_axis=0, concat_axis=0, tiled=True)
    back, predictions = call(
        sum_kernel,
        (shape(TILES, 16, 128, dtype=BF16), shape(2, n_t)),
        limit=24,
    )(got, perm, tg_tile, tg_rank)
    summed = lax.all_to_all(back, axes, split_axis=0, concat_axis=0, tiled=True)
    grad_first, grad_second, grad_lift, grad_out = call(
        final_kernel,
        (shape(64, 1600), shape(64, 1600), shape(13, 64), shape(2, 64)),
        scratch=[pltpu.VMEM((TILES, 16, 128), F32)],
        limit=24,
    )(summed)
    return predictions, grad_lift, grad_first, grad_second, grad_out.T


def solution(mesh):
    placed = (
        P(("lat", "lon"), None),
        P(("lat", "lon")),
        P(None, ("lat", "lon")),
        P(None, ("lat", "lon")),
        P(None, "lat", "lon"),
        P(("lat", "lon"), None),
        P(("lat", "lon")),
        P(None, ("lat", "lon")),
        P(),
        P(),
        P(),
        P(),
        P(None, ("lat", "lon")),
    )
    return jax.shard_map(
        shards,
        mesh=mesh,
        in_specs=placed,
        out_specs=(P(None, ("lat", "lon")), P(), P(), P(), P()),
        check_vma=False,
    )
```
